256 devices in a mesh: seq: 32 (over x, y, core), dp: 8 (over z).
Axes of the slice: x: 4, y: 4, z: 8, core: 2. Of those that a mesh axis runs over, the one named last changes fastest.
Arguments:
- frame_counts: int32 [8, 16], P('dp'), may hold values from 1 to 3072, 6144 in all within a row
- glu_out: bfloat16 [8, 6144, 1536], P('dp', 'seq'), may hold values from -40 to 40
- tap_weight: float32 [32, 1536], replicated, may hold values from -1 to 1
- bn_gain: float32 [1536], replicated, may hold values from 0.1 to 1.9
- bn_shift: float32 [1536], replicated, may hold values from -3 to 3
- proj_weight: bfloat16 [1536, 1536], replicated, may hold values from -0.15625 to 0.15625
- out_grad: bfloat16 [8, 6144, 1536], P('dp', 'seq'), may hold values from -6 to 6
Outputs:
- block_out: bfloat16 [8, 6144, 1536], P('dp', 'seq')
- frame_grad: bfloat16 [8, 6144, 1536], P('dp', 'seq')
- tap_grad: float32 [32, 1536], replicated
- gain_grad: float32 [1536], replicated
- shift_grad: float32 [1536], replicated
- proj_grad: float32 [1536, 1536], P(('seq', 'dp'))
The draws below stay inside these ranges and needn't reach their ends.
Inputs may be any that keep to these rules, and one draw needn't show every extreme that they name: `frame_counts`: each row sums to 6144; the utterances lie one after another along the group's frames.
All inputs are finite; a program needn't handle non-finite values.
Results may differ from the reference program's by a relative error of at most 0.0049.
Values may be sent and summed in bfloat16 or wider, within the bound.
No kernel may reach another device: no remote copies, remote signals or barrier semaphores. Data moves between devices by JAX's collectives and lax.ppermute only.
A program may use at most 128 MiB of HBM per device.

```python
import math
import jax
import jax.numpy as jnp
import numpy as np
from jax import lax

D = 1536
KERNEL = 32
HALF = 16
UTT = 16
GROUPS = 8
FS = 6144


def draw_glu_out(key, part):
    key = jax.random.fold_in(key, 11)
    key_base, key_rows, key_cols = jax.random.split(key, 3)
    trend = jnp.exp(math.log(3.0) * jnp.arange(FS, dtype=jnp.float32) / FS)[None, :, None]
    rows = jnp.exp(jax.random.uniform(key_rows, (GROUPS, FS, 1), jnp.float32, 0.0, math.log(10.0))) * trend
    cols = jnp.exp(jax.random.uniform(key_cols, (1, 1, D), jnp.float32, 0.0, math.log(10.0)))
    base = jnp.clip(jax.random.normal(key_base, (GROUPS, FS, D), jnp.float32), -4.0, 4.0)
    return (base * rows * cols / 30.0).astype(jnp.bfloat16)


def shard_levels(own_key, dims, pieces, low, top_value):
    level, own = 1.0, jax.random.fold_in(own_key, 6)
    for axis_at, parts in pieces:
        heights = jnp.exp(jax.random.uniform(jax.random.fold_in(own, axis_at), (parts,), jnp.float32, low / len(pieces), top_value / len(pieces)))
        level = level * jnp.repeat(heights, dims[axis_at] // parts).reshape([-1 if axis == axis_at else 1 for axis in range(len(dims))])
    return level


def profile(number_of, total, bound, lean):
    weights = [(1 << 20) // math.isqrt(grade ** lean) + 1 for grade in range(2, number_of + 1)]
    spare, given = total - bound - (number_of - 1), [1] * (number_of - 1)
    while spare > 0:
        candidates = [i for i in range(number_of - 1) if given[i] < bound]
        whole, remaining = sum([weights[i] for i in candidates]), spare
        for i in candidates:
            extra = min(bound - given[i], max(1, remaining * weights[i] // whole), spare)
            given[i] = given[i] + extra
            spare = spare - extra
    return np.array([bound] + given)


def ragged_sizes(stream_key, amount, total, reach, skew):
    if amount == 2:
        one = jax.random.randint(stream_key, (), max(1, total - reach), min(reach, total - 1) + 1)
        return jnp.stack([one, total - one])
    sizes = jnp.asarray(profile(amount, total, reach, skew), jnp.int32)
    couples = (amount - 1) // 2
    source_of, receiver = sizes[1:1 + 2 * couples:2], sizes[2:2 + 2 * couples:2]
    margin = jnp.minimum(source_of - 1, reach - receiver)
    shifted = jax.random.randint(jax.random.fold_in(stream_key, 1), (couples,), 0, 1 << 20) % (margin + 1)
    sizes = sizes.at[1:1 + 2 * couples:2].set(source_of - shifted).at[2:2 + 2 * couples:2].set(receiver + shifted)
    return sizes[jax.random.permutation(jax.random.fold_in(stream_key, 2), amount)]


def noise(key, dims, spread, bound, cuts=(), held_as=jnp.bfloat16):
    result = jax.random.normal(key, dims, jnp.float32) * spread
    if len(cuts) > 0:
        result = shard_levels(key, dims, cuts, -0.22, 0.18) * result
    return jnp.clip(result, min=-bound, max=bound).astype(held_as)


def setup_inputs(seed: int = 0) -> dict:
    key_of = jax.random.split(jax.random.key(seed), 8)
    frame_counts = jax.vmap(lambda own: ragged_sizes(own, UTT, FS, FS // 2, 2))(jax.random.split(key_of[0], GROUPS)).reshape((GROUPS, UTT)).astype(jnp.int32)
    glu_out = draw_glu_out(jax.random.fold_in(key_of[7], 71), 0)
    tap_weight = noise(key_of[2], (KERNEL, D), KERNEL ** -0.5, 1.0, (), jnp.float32)
    bn_gain = jnp.clip(1.0 + 0.18 * jax.random.normal(key_of[3], (D,), jnp.float32), 0.1, 1.9)
    bn_shift = noise(key_of[4], (D,), 0.5, 3.0, (), jnp.float32)
    proj_weight = noise(key_of[5], (D, D), D ** -0.5, 0.15625)
    out_grad = noise(key_of[6], (GROUPS, FS, D), 1.0, 6.0, ((0, 8), (1, 32)))
    return {"frame_counts": frame_counts, "glu_out": glu_out, "tap_weight": tap_weight, "bn_gain": bn_gain, "bn_shift": bn_shift, "proj_weight": proj_weight, "out_grad": out_grad}


EPSILON = 1e-05

def segment_ids(counts, positions):
    ends = jnp.cumsum(counts.astype(jnp.int32)).astype(jnp.int32)
    return lax.optimization_barrier(jnp.sum((positions[:, None] >= ends[None, :]).astype(jnp.int32), axis=1)).astype(jnp.int32)

def tap_masks(segments, frames, width):
    centre = segments[width:width + frames]
    return [(segments[column:column + frames] == centre).astype(jnp.float32)[:, None] for column in range(2 * width)]

def depthwise(padded, taps, masks, frames):
    total = jnp.zeros((frames, padded.shape[1]), jnp.float32)
    for column in range(len(masks)):
        total = total + taps[column][None, :] * padded[column:column + frames].astype(jnp.float32) * masks[column]
    return total

def transpose_conv(padded_grad, taps, segments, frames, width):
    centre = segments[width:width + frames]
    total = jnp.zeros((frames, padded_grad.shape[1]), jnp.float32)
    for column in range(2 * width):
        anchor = 2 * width - column
        keep = (segments[anchor:anchor + frames] == centre).astype(jnp.float32)[:, None]
        total = total + taps[column][None, :] * padded_grad[anchor:anchor + frames] * keep
    return total

def group_forward(inputs, counts, taps):
    frames = inputs.shape[0]
    padded = jnp.pad(inputs, ((HALF, HALF), (0, 0)))
    positions = jnp.arange(frames + 2 * HALF, dtype=jnp.int32) - HALF
    segments = segment_ids(counts, positions)
    masks = tap_masks(segments, frames, HALF)
    return (depthwise(padded, taps, masks, frames), padded, masks, segments)

def reference(frame_counts, glu_out, tap_weight, bn_gain, bn_shift, proj_weight, out_grad):
    frames = glu_out.shape[1]
    total_rows = glu_out.shape[0] * frames

    def sum_pass(item):
        return lax.optimization_barrier(jnp.sum(group_forward(item[0], item[1], tap_weight)[0], axis=0))
    mean = lax.optimization_barrier(jnp.sum(lax.map(sum_pass, (glu_out, frame_counts)), axis=0)) / total_rows

    def spread_pass(item):
        centred = group_forward(item[0], item[1], tap_weight)[0] - mean
        return lax.optimization_barrier(jnp.sum(centred * centred, axis=0))
    var = lax.optimization_barrier(jnp.sum(lax.map(spread_pass, (glu_out, frame_counts)), axis=0)) / total_rows
    inverse = lax.rsqrt(var + EPSILON)

    def main_pass(item):
        inputs, counts, grads_in = item
        conv = group_forward(inputs, counts, tap_weight)[0]
        normed = (conv - mean) * inverse
        act = bn_gain * normed + bn_shift
        gate_value = jax.nn.sigmoid(act)
        swished = (act * gate_value).astype(jnp.bfloat16)
        block = jnp.dot(swished, proj_weight, preferred_element_type=jnp.float32).astype(jnp.bfloat16)
        back = lax.dot_general(grads_in, proj_weight, (((1,), (1,)), ((), ())), preferred_element_type=jnp.float32)
        act_grad = back * gate_value * (1.0 + act * (1.0 - gate_value))
        weight_part = lax.dot_general(swished, grads_in, (((0,), (0,)), ((), ())), preferred_element_type=jnp.float32)
        return (block, act_grad, lax.optimization_barrier(jnp.sum(act_grad, axis=0)), lax.optimization_barrier(jnp.sum(act_grad * normed, axis=0)), weight_part)
    block_out, act_grads, shift_parts, gain_parts, weight_parts = lax.map(main_pass, (glu_out, frame_counts, out_grad))
    shift_grad = lax.optimization_barrier(jnp.sum(shift_parts, axis=0))
    gain_grad = lax.optimization_barrier(jnp.sum(gain_parts, axis=0))
    proj_grad = lax.optimization_barrier(jnp.sum(weight_parts, axis=0))

    def back_pass(item):
        inputs, counts, act_grad = item
        conv, padded, masks, segments = group_forward(inputs, counts, tap_weight)
        normed = (conv - mean) * inverse
        conv_grad = bn_gain * inverse * (act_grad - shift_grad / total_rows - normed * gain_grad / total_rows)
        tap_part = jnp.stack([lax.optimization_barrier(jnp.sum(conv_grad * padded[column:column + frames].astype(jnp.float32) * masks[column], axis=0)) for column in range(2 * HALF)])
        padded_grad = jnp.pad(conv_grad, ((HALF, HALF), (0, 0)))
        grad_frames = transpose_conv(padded_grad, tap_weight, segments, frames, HALF).astype(jnp.bfloat16)
        return (grad_frames, tap_part)
    frame_grad, tap_parts = lax.map(back_pass, (glu_out, frame_counts, act_grads))
    tap_grad = lax.optimization_barrier(jnp.sum(tap_parts, axis=0))
    return (block_out, frame_grad, tap_grad, gain_grad, shift_grad, proj_grad)
```

```python
import jax
import jax.numpy as jnp
from jax import lax
from jax.sharding import Mesh, PartitionSpec as P

HALF = 16
KERNEL = 2 * HALF
EPSILON = 1e-05
SEQ = ("x", "y", "c")
PLANE = ("x", "y")
COLUMN = ("c", "z")


def shifted(value, axes, step):
    count = lax.axis_size(axes)
    pairs = [(i, i + step) for i in range(count) if 0 <= i + step < count]
    return lax.ppermute(value, axes, pairs)


def swapped(value):
    return lax.ppermute(value, "c", [(0, 1), (1, 0)])


def exchanged(blocks, axes):
    return lax.all_to_all(blocks, axes, 0, 0, tiled=True)


def gathered(value, axes):
    count = lax.axis_size(axes)
    return exchanged(jnp.broadcast_to(value[None], (count,) + value.shape), axes)


def summed(value):
    value = jnp.sum(gathered(value, PLANE), axis=0)
    return jnp.sum(gathered(value, COLUMN), axis=0)


def merged(stats, count):
    means, squares = stats[:, 0], stats[:, 1]
    mean = jnp.mean(means, axis=0)
    spread = jnp.sum(jnp.square(means - mean), axis=0)
    return jnp.stack([mean, jnp.sum(squares, axis=0) + count * spread])


def segment_ids(counts, positions, frames):
    ends = jnp.cumsum(counts)
    found = jnp.sum((positions[:, None] >= ends[None, :]).astype(jnp.int32), axis=1)
    return jnp.where((positions >= 0) & (positions < frames), found, -1)


def local(frame_counts, glu_out, tap_weight, bn_gain, bn_shift, proj_weight, out_grad):
    inputs = glu_out[0]
    grads_in = out_grad[0]
    frames, width = inputs.shape
    half_width = width // 2
    devices = lax.axis_size(SEQ)
    total_rows = frames * devices * lax.axis_size("z")
    core = lax.axis_index("c")

    up = jnp.concatenate([inputs[-2 * HALF :], grads_in[-HALF:]])
    down = jnp.concatenate([inputs[: 2 * HALF], grads_in[:HALF]])
    low, high = shifted(up, SEQ, 1), shifted(down, SEQ, -1)
    wide = jnp.concatenate([low[: 2 * HALF], inputs, high[: 2 * HALF]]).astype(jnp.float32)
    grads_wide = jnp.concatenate([low[2 * HALF :], grads_in, high[2 * HALF :]])

    mine = lax.dynamic_slice_in_dim(grads_in, core * half_width, half_width, 1)
    other = swapped(lax.dynamic_slice_in_dim(grads_in, (1 - core) * half_width, half_width, 1))

    first = lax.axis_index(SEQ) * frames - 2 * HALF
    positions = first + jnp.arange(frames + 4 * HALF, dtype=jnp.int32)
    segments = segment_ids(frame_counts[0], positions, frames * devices)
    rows = frames + 2 * HALF
    centre = segments[HALF : HALF + rows]

    conv = jnp.zeros((rows, width), jnp.float32)
    for k in range(KERNEL):
        keep = (segments[k : k + rows] == centre)[:, None]
        conv = conv + tap_weight[k][None, :] * jnp.where(keep, wide[k : k + rows], 0.0)

    inner = conv[HALF : HALF + frames]
    mean = jnp.mean(inner, axis=0)
    stats = jnp.stack([mean, jnp.sum(jnp.square(inner - mean), axis=0)])
    stats = merged(gathered(stats, PLANE), frames)
    stats = merged(gathered(stats, COLUMN), frames * lax.axis_size(PLANE))
    mean, var = stats[0], stats[1] / total_rows

    inverse = lax.rsqrt(var + EPSILON)
    normed = (conv - mean) * inverse
    act = bn_gain * normed + bn_shift
    gate = jax.nn.sigmoid(act)
    swished = (act * gate)[HALF : HALF + frames].astype(jnp.bfloat16)
    block = jnp.dot(swished, proj_weight, preferred_element_type=jnp.float32).astype(jnp.bfloat16)
    back = lax.dot_general(
        grads_wide, proj_weight, (((1,), (1,)), ((), ())), preferred_element_type=jnp.float32
    )
    act_grad = back * gate * (1.0 + act * (1.0 - gate))

    inner_grad, inner_normed = act_grad[HALF : HALF + frames], normed[HALF : HALF + frames]
    sums = jnp.stack([jnp.sum(inner_grad, axis=0), jnp.sum(inner_grad * inner_normed, axis=0)])
    shift_grad, gain_grad = summed(sums)

    pair = jnp.concatenate([swished, swapped(swished)])
    part = lax.dot_general(
        pair, jnp.concatenate([mine, other]), (((0,), (0,)), ((), ())),
        preferred_element_type=jnp.float32,
    ).astype(jnp.bfloat16)
    chips = lax.axis_size(PLANE)
    part = exchanged(part.reshape(chips, width // chips, half_width), PLANE)
    part = jnp.sum(part.astype(jnp.float32), axis=0)
    column = lax.axis_size(COLUMN)
    part = exchanged(part.reshape(column, -1, half_width), COLUMN)
    part = jnp.sum(part.reshape((2, column // 2) + part.shape[1:]), axis=1)
    proj_grad = jnp.concatenate([part[0], part[1]], axis=1)

    conv_grad = (
        bn_gain * inverse * (act_grad - shift_grad / total_rows - normed * gain_grad / total_rows)
    )
    inner_grad = conv_grad[HALF : HALF + frames]
    inner_ids = centre[HALF : HALF + frames]
    taps = []
    total = jnp.zeros((frames, width), jnp.float32)
    for k in range(KERNEL):
        keep = (centre[k : k + frames] == inner_ids)[:, None]
        taps.append(jnp.sum(inner_grad * jnp.where(keep, wide[HALF + k : HALF + k + frames], 0.0), axis=0))
        anchor = KERNEL - k
        keep = (centre[anchor : anchor + frames] == inner_ids)[:, None]
        total = total + tap_weight[k][None, :] * jnp.where(keep, conv_grad[anchor : anchor + frames], 0.0)
    frame_grad = total.astype(jnp.bfloat16)
    taps = jnp.stack(taps).reshape(chips, KERNEL // chips, width)
    taps = jnp.sum(exchanged(taps, PLANE), axis=0)
    taps = jnp.sum(gathered(taps, COLUMN), axis=0)
    tap_grad = gathered(taps, PLANE).reshape(KERNEL, width)
    return (block[None], frame_grad[None], tap_grad, gain_grad, shift_grad, proj_grad)


def solution(mesh):
    grid = Mesh(mesh.devices.reshape(4, 4, 2, -1), ("x", "y", "c", "z"))
    wide = P("z", SEQ, None)
    return jax.shard_map(
        local,
        mesh=grid,
        in_specs=(P("z", None), wide, P(), P(), P(), P(), wide),
        out_specs=(wide, wide, P(), P(), P(), P(("x", "y", "c", "z"), None)),
        check_vma=False,
    )
```

```python
import jax
import jax.numpy as jnp
from jax import lax
from jax.experimental import pallas as pl
from jax.experimental.pallas import tpu as pltpu
from jax.sharding import Mesh, PartitionSpec as P

HALF = 16
KERNEL = 2 * HALF
EPSILON = 1e-05
SEQ = ("x", "y", "c")
PLANE = ("x", "y")
COLUMN = ("c", "z")
LANES = 128
TILE = 512
SUB = 8
BLOCKS = 4
GROUP = 4
F32 = jnp.float32


def shifted(value, axes, step):
    count = lax.axis_size(axes)
    pairs = [(i, i + step) for i in range(count) if 0 <= i + step < count]
    return lax.ppermute(value, axes, pairs)


def rotated(value, axis, step):
    count = lax.axis_size(axis)
    return lax.ppermute(value, axis, [(i, (i + step) % count) for i in range(count)])


def exchanged(blocks, axes):
    return lax.all_to_all(blocks, axes, 0, 0, tiled=True)


def gathered(value, axes):
    count = lax.axis_size(axes)
    return exchanged(jnp.broadcast_to(value[None], (count,) + value.shape), axes)


def merged(stats, count):
    means, squares = stats[:, 0], stats[:, 1]
    mean = jnp.mean(means, axis=0)
    spread = jnp.sum(jnp.square(means - mean), axis=0)
    return jnp.stack([mean, jnp.sum(squares, axis=0) + count * spread])


def segment_ids(counts, positions, frames):
    ends = jnp.cumsum(counts)
    found = jnp.sum((positions[:, None] >= ends[None, :]).astype(jnp.int32), axis=1)
    return jnp.where((positions >= 0) & (positions < frames), found, -1)


def window_mask(counts, first, frames, limit):
    row = lax.broadcasted_iota(jnp.int32, (KERNEL, frames + 4 * HALF), 1)
    owner = row + HALF - lax.broadcasted_iota(jnp.int32, row.shape, 0)
    ends = jnp.cumsum(counts)[:, None, None]
    same = jnp.all((first + row >= ends) == (first + owner >= ends), axis=0)
    inside = (owner >= 2 * HALF) & (owner < 2 * HALF + frames)
    valid = (first + row >= 0) & (first + row < limit)
    return (same & inside & valid).astype(jnp.bfloat16)


def shift_copies(source, copies):
    rows = copies.shape[1]
    for b in range(SUB):
        copies[b] = source[b : b + rows]


def lane_groups():
    tiles = [pl.ds(t * LANES, LANES) for t in range(TILE // LANES)]
    return [tiles[t : t + GROUP] for t in range(0, len(tiles), GROUP)]


def convolve(ids_ref, ids, copies, taps_ref, out_ref, rows, centre, tap_of, id_shift):
    offsets = [o for o in range(KERNEL + 1) if 0 <= tap_of(o) < KERNEL]
    for tiles in lane_groups():
        def step(j, carry, tiles=tiles):
            base = pl.multiple_of(j * SUB * BLOCKS, SUB * BLOCKS)
            own = [ids_ref[pl.ds(base + i * SUB + centre, SUB), :] for i in range(BLOCKS)]
            totals = [[jnp.zeros((SUB, LANES), F32) for _ in tiles] for _ in range(BLOCKS)]
            for low in range(SUB):
                steps = [o // SUB for o in offsets if o % SUB == low]
                reads = range(min(steps), max(steps) + BLOCKS)
                near = {i: ids[low, pl.ds(base + i * SUB + id_shift, SUB), :] for i in reads}
                keep = {(a, i): near[a + i] == own[i] for a in steps for i in range(BLOCKS)}
                for t, lanes in enumerate(tiles):
                    value = {i: copies[low, pl.ds(base + i * SUB, SUB), lanes] for i in reads}
                    for a in steps:
                        tap = taps_ref[pl.ds(tap_of(a * SUB + low), 1), lanes]
                        for i in range(BLOCKS):
                            term = jnp.where(keep[a, i], value[a + i], 0.0)
                            totals[i][t] = totals[i][t] + tap * term
            for i in range(BLOCKS):
                for t, lanes in enumerate(tiles):
                    out_ref[pl.ds(base + i * SUB, SUB), lanes] = totals[i][t]
            return carry

        lax.fori_loop(0, rows // (SUB * BLOCKS), step, 0)


def correlate(grad_ref, ids_ref, ids, copies, rows, first, out_ref):
    steps = range(KERNEL // SUB)
    for tiles in lane_groups():
        for low in range(SUB):
            def step(j, sums, tiles=tiles, low=low):
                base = pl.multiple_of(j * SUB * BLOCKS, SUB * BLOCKS)
                reads = range(len(steps) + BLOCKS - 1)
                own = [ids_ref[pl.ds(base + i * SUB + first + HALF, SUB), :] for i in range(BLOCKS)]
                near = [ids[low, pl.ds(base + i * SUB + first, SUB), :] for i in reads]
                keep = {(a, i): near[a + i] == own[i] for a in steps for i in range(BLOCKS)}
                out = list(sums)
                for t, lanes in enumerate(tiles):
                    value = [copies[low, pl.ds(base + i * SUB + first, SUB), lanes] for i in reads]
                    grads = [grad_ref[pl.ds(base + i * SUB, SUB), lanes] for i in range(BLOCKS)]
                    for a in steps:
                        at = t * len(steps) + a
                        for i in range(BLOCKS):
                            out[at] = out[at] + jnp.where(keep[a, i], value[a + i], 0.0) * grads[i]
                return tuple(out)

            start = tuple(jnp.zeros((SUB, LANES), F32) for _ in range(len(steps) * len(tiles)))
            sums = lax.fori_loop(0, rows // (SUB * BLOCKS), step, start)
            for t, lanes in enumerate(tiles):
                for a in steps:
                    total = jnp.sum(sums[t * len(steps) + a], axis=0, keepdims=True)
                    out_ref[pl.ds(a * SUB + low, 1), lanes] = total


def conv_kernel(wide_ref, ids_ref, taps_ref, conv_ref, stats_ref, copies, ids):
    rows = conv_ref.shape[0]

    @pl.when(pl.program_id(0) == 0)
    def _():
        shift_copies(ids_ref[...], ids)

    shift_copies(wide_ref[...].astype(F32), copies)

    convolve(ids_ref, ids, copies, taps_ref, conv_ref, rows, HALF, lambda o: o, 0)
    inner = conv_ref[HALF : rows - HALF, :]
    mean = jnp.sum(inner, axis=0, keepdims=True) / inner.shape[0]
    stats_ref[0:1, :] = mean
    stats_ref[1:2, :] = jnp.sum(jnp.square(inner - mean), axis=0, keepdims=True)


def moments_kernel(wide_ref, ids_ref, conv_ref, stats_ref, out_ref, copies, ids, centred):
    rows = conv_ref.shape[0] - 2 * HALF

    @pl.when(pl.program_id(0) == 0)
    def _():
        shift_copies(ids_ref[...], ids)

    shift_copies(wide_ref[...].astype(F32), copies)
    centred[...] = conv_ref[HALF : HALF + rows, :] - stats_ref[0:1, :]
    correlate(centred, ids_ref, ids, copies, rows, HALF, out_ref)


def act_kernel(
    wide_ref, ids_ref, conv_ref, back_ref, chan_ref, swished_ref, grad_ref, sums_ref, taps_ref, copies, ids,
    centred,
):
    rows = conv_ref.shape[0] - 2 * HALF

    @pl.when(pl.program_id(0) == 0)
    def _():
        shift_copies(ids_ref[...], ids)

    shift_copies(wide_ref[...].astype(F32), copies)
    mean, inverse, gain, shift = (chan_ref[i : i + 1, :] for i in range(4))
    normed = (conv_ref[...] - mean) * inverse
    act = gain * normed + shift
    gate = jax.nn.sigmoid(act)
    grad = back_ref[...] * gate * (1.0 + act * (1.0 - gate))
    grad_ref[...] = grad
    swished_ref[...] = (act * gate)[HALF : HALF + rows].astype(jnp.bfloat16)
    inner, inner_normed = grad[HALF : HALF + rows], normed[HALF : HALF + rows]
    sums_ref[0:1, :] = jnp.sum(inner, axis=0, keepdims=True)
    sums_ref[1:2, :] = jnp.sum(inner * inner_normed, axis=0, keepdims=True)
    centred[...] = inner
    correlate(centred, ids_ref, ids, copies, rows, HALF, taps_ref)


def frame_kernel(ids_ref, conv_ref, grad_ref, chan_ref, taps_ref, out_ref, copies, ids, result):
    rows = out_ref.shape[0]

    @pl.when(pl.program_id(0) == 0)
    def _():
        shift_copies(ids_ref[...], ids)

    mean, inverse, scale, shift, slope = (chan_ref[i : i + 1, :] for i in range(5))
    normed = (conv_ref[...] - mean) * inverse
    grad = scale * (grad_ref[...] - shift - normed * slope)
    for b in range(SUB):
        count = rows + 2 * HALF - (SUB if b else 0)
        copies[b, 0:count, :] = grad[b : b + count]

    convolve(
        ids_ref, ids, copies, taps_ref, result, rows, 2 * HALF, lambda o: KERNEL - o, HALF
    )
    out_ref[...] = result[...].astype(jnp.bfloat16)


def columns(rows):
    return pl.BlockSpec((rows, TILE), lambda i: (0, i))


def call(kernel, width, ins, outs, scratch, weight):
    specs = [
        pl.BlockSpec(a.shape, lambda i: (0, 0)) if a.dtype == jnp.int32 else columns(a.shape[0])
        for a in ins
    ]
    return pl.pallas_call(
        kernel,
        grid=(width // TILE,),
        in_specs=specs,
        out_specs=[columns(rows) for rows, _ in outs],
        out_shape=[jax.ShapeDtypeStruct((rows, width), kind) for rows, kind in outs],
        scratch_shapes=scratch,
        compiler_params=pltpu.CompilerParams(vmem_limit_bytes=32 * 1024 * 1024),
        cost_estimate=pl.CostEstimate(
            flops=weight * 192 * KERNEL * width * 4, bytes_accessed=4 * 224 * width * 4, transcendentals=0
        ),
    )(*ins)


def local(frame_counts, glu_out, tap_weight, bn_gain, bn_shift, proj_weight, out_grad):
    inputs = glu_out[0]
    grads_in = out_grad[0]
    frames, width = inputs.shape
    half_width = width // 2
    devices = lax.axis_size(SEQ)
    total_rows = frames * devices * lax.axis_size("z")
    core = lax.axis_index("c")

    up = jnp.concatenate([inputs[-2 * HALF :], grads_in[-HALF:]])
    down = jnp.concatenate([inputs[: 2 * HALF], grads_in[:HALF]])
    low, high = shifted(up, SEQ, 1), shifted(down, SEQ, -1)
    wide = jnp.concatenate([low[: 2 * HALF], inputs, high[: 2 * HALF]])
    grads_wide = jnp.concatenate([low[2 * HALF :], grads_in, high[2 * HALF :]])

    mine = lax.dynamic_slice_in_dim(grads_in, core * half_width, half_width, 1)
    other = lax.dynamic_slice_in_dim(grads_in, (1 - core) * half_width, half_width, 1)
    cotangents = jnp.concatenate([mine, rotated(other, "c", 1)])

    first = lax.axis_index(SEQ) * frames - 2 * HALF
    positions = first + jnp.arange(frames + 4 * HALF, dtype=jnp.int32)
    segments = segment_ids(frame_counts[0], positions, frames * devices)
    segments = jnp.broadcast_to(segments[:, None], (frames + 4 * HALF, LANES))
    rows = frames + 2 * HALF
    reach = frames + 4 * HALF - SUB
    value_copies = pltpu.VMEM((SUB, reach, TILE), F32)
    id_copies = pltpu.VMEM((SUB, reach, LANES), jnp.int32)

    conv, own_stats = call(
        conv_kernel, width, [wide, segments, tap_weight], [(rows, F32), (2, F32)],
        [value_copies, id_copies], 1,
    )
    back = lax.dot_general(
        grads_wide, proj_weight, (((1,), (1,)), ((), ())), preferred_element_type=F32
    )
    (product,) = call(
        moments_kernel, width, [wide, segments, conv, own_stats], [(KERNEL, F32)],
        [value_copies, id_copies, pltpu.VMEM((frames, TILE), F32)], 1,
    )
    plain = jnp.dot(
        window_mask(frame_counts[0], first, frames, frames * devices), wide, preferred_element_type=F32
    )
    stats = merged(gathered(own_stats, PLANE), frames)
    stats = merged(gathered(stats, COLUMN), frames * lax.axis_size(PLANE))
    mean, var = stats[0], stats[1] / total_rows
    inverse = lax.rsqrt(var + EPSILON)

    swished, act_grad, sums, taps = call(
        act_kernel, width,
        [wide, segments, conv, back, jnp.stack([mean, inverse, bn_gain, bn_shift])],
        [(frames, jnp.bfloat16), (rows, F32), (2, F32), (KERNEL, F32)],
        [value_copies, id_copies, pltpu.VMEM((frames, TILE), F32)], 1,
    )

    product = inverse * (product + (own_stats[0] - mean) * plain)
    chips = lax.axis_size(PLANE)
    each = KERNEL // chips
    parts = jnp.stack([taps, plain, product]).reshape(3, chips, each, width)
    parts = jnp.swapaxes(parts, 0, 1).reshape(chips, 3 * each, width)
    parts = jnp.concatenate([parts, jnp.broadcast_to(sums[None], (chips, 2, width))], axis=1)
    parts = jnp.sum(exchanged(parts, PLANE), axis=0)
    parts = jnp.sum(gathered(parts, COLUMN), axis=0)
    shift_grad, gain_grad = parts[3 * each], parts[3 * each + 1]
    scale = bn_gain * inverse
    shift_mean, gain_mean = shift_grad / total_rows, gain_grad / total_rows
    taps, plain, product = parts[:each], parts[each : 2 * each], parts[2 * each : 3 * each]
    tap_rows = scale * (taps - shift_mean * plain - gain_mean * product)

    pair = jnp.concatenate([swished, rotated(swished, "c", 1)])
    part = lax.dot_general(
        pair, cotangents, (((0,), (0,)), ((), ())), preferred_element_type=F32
    ).astype(jnp.bfloat16)
    terms, rest = [], tap_rows
    for _ in range(3):
        term = lax.reduce_precision(rest, 8, 7)
        terms.append(term.astype(jnp.bfloat16))
        rest = rest - term
    each_rows = width // chips
    terms = jnp.stack(terms).reshape(-1, half_width)
    used = terms.shape[0]
    terms = jnp.pad(terms, ((0, -used % 16), (0, 0)))
    part = jnp.concatenate(
        [part.reshape(chips, each_rows, half_width), jnp.broadcast_to(terms[None], (chips,) + terms.shape)], axis=1
    )
    part = exchanged(part, PLANE)
    tap_grad = part[:, each_rows : each_rows + used].astype(F32).reshape(chips, 3, each, width)
    tap_grad = jnp.sum(tap_grad, axis=1).reshape(KERNEL, width)
    part = jnp.sum(part[:, :each_rows].astype(F32), axis=0)
    column = lax.axis_size(COLUMN)
    part = exchanged(part.reshape(column, -1, half_width), COLUMN)
    part = jnp.sum(part.reshape((2, column // 2) + part.shape[1:]), axis=1)
    proj_grad = jnp.concatenate([part[0], part[1]], axis=1)

    block = jnp.dot(swished, proj_weight, preferred_element_type=F32).astype(jnp.bfloat16)

    (frame_grad,) = call(
        frame_kernel, width,
        [segments, conv, act_grad, jnp.stack([mean, inverse, scale, shift_mean, gain_mean]), tap_weight],
        [(frames, jnp.bfloat16)],
        [value_copies, id_copies, pltpu.VMEM((frames, TILE), F32)], 1,
    )
    return (block[None], frame_grad[None], tap_grad, gain_grad, shift_grad, proj_grad)


def solution(mesh):
    grid = Mesh(mesh.devices.reshape(4, 4, 2, -1), ("x", "y", "c", "z"))
    wide = P("z", SEQ, None)
    return jax.shard_map(
        local,
        mesh=grid,
        in_specs=(P("z", None), wide, P(), P(), P(), P(), wide),
        out_specs=(wide, wide, P(), P(), P(), P(("x", "y", "c", "z"), None)),
        check_vma=False,
    )
```

```python
import functools

import jax
import jax.numpy as jnp
from jax import lax
from jax.experimental import pallas as pl
from jax.experimental.pallas import tpu as pltpu
from jax.sharding import Mesh, PartitionSpec as P

HALF = 16
KERNEL = 2 * HALF
EPSILON = 1e-05
SEQ = ("x", "y", "c")
PLANE = ("x", "y")
COLUMN = ("c", "z")
LANES = 128
TILE = 512
SUB = 8
BLOCKS = 4
GROUP = 4
F32 = jnp.float32


def shifted(value, axes, step):
    count = lax.axis_size(axes)
    pairs = [(i, i + step) for i in range(count) if 0 <= i + step < count]
    return lax.ppermute(value, axes, pairs)


def rotated(value, axis, step):
    count = lax.axis_size(axis)
    return lax.ppermute(value, axis, [(i, (i + step) % count) for i in range(count)])


def exchanged(blocks, axes):
    return lax.all_to_all(blocks, axes, 0, 0, tiled=True)


def gathered(value, axes):
    count = lax.axis_size(axes)
    return exchanged(jnp.broadcast_to(value[None], (count,) + value.shape), axes)


def merged(stats, count):
    means, squares = stats[:, 0], stats[:, 1]
    mean = jnp.mean(means, axis=0)
    spread = jnp.sum(jnp.square(means - mean), axis=0)
    return jnp.stack([mean, jnp.sum(squares, axis=0) + count * spread])


def segment_ids(counts, positions, frames):
    ends = jnp.cumsum(counts)
    found = jnp.sum((positions[:, None] >= ends[None, :]).astype(jnp.int32), axis=1)
    return jnp.where((positions >= 0) & (positions < frames), found, -1)


def window_mask(counts, first, frames, limit):
    row = lax.broadcasted_iota(jnp.int32, (KERNEL, frames + 4 * HALF), 1)
    owner = row + HALF - lax.broadcasted_iota(jnp.int32, row.shape, 0)
    ends = jnp.cumsum(counts)[:, None, None]
    same = jnp.all((first + row >= ends) == (first + owner >= ends), axis=0)
    inside = (owner >= 2 * HALF) & (owner < 2 * HALF + frames)
    valid = (first + row >= 0) & (first + row < limit)
    return (same & inside & valid).astype(jnp.bfloat16)


def shift_copies(source, copies):
    rows = copies.shape[1]
    for b in range(SUB):
        copies[b] = source[b : b + rows]


def lane_groups():
    tiles = [pl.ds(t * LANES, LANES) for t in range(TILE // LANES)]
    return [tiles[t : t + GROUP] for t in range(0, len(tiles), GROUP)]


def convolve(ids_ref, ids, copies, taps_ref, out_ref, rows, centre, tap_of, id_shift):
    offsets = [o for o in range(KERNEL + 1) if 0 <= tap_of(o) < KERNEL]
    for tiles in lane_groups():
        def step(j, carry, tiles=tiles):
            base = pl.multiple_of(j * SUB * BLOCKS, SUB * BLOCKS)
            own = [ids_ref[pl.ds(base + i * SUB + centre, SUB), :] for i in range(BLOCKS)]
            totals = [[jnp.zeros((SUB, LANES), F32) for _ in tiles] for _ in range(BLOCKS)]
            for low in range(SUB):
                steps = [o // SUB for o in offsets if o % SUB == low]
                reads = range(min(steps), max(steps) + BLOCKS)
                near = {i: ids[low, pl.ds(base + i * SUB + id_shift, SUB), :] for i in reads}
                keep = {(a, i): near[a + i] == own[i] for a in steps for i in range(BLOCKS)}
                for t, lanes in enumerate(tiles):
                    value = {i: copies[low, pl.ds(base + i * SUB, SUB), lanes] for i in reads}
                    for a in steps:
                        tap = taps_ref[pl.ds(tap_of(a * SUB + low), 1), lanes]
                        for i in range(BLOCKS):
                            term = jnp.where(keep[a, i], value[a + i], 0.0)
                            totals[i][t] = totals[i][t] + tap * term
            for i in range(BLOCKS):
                for t, lanes in enumerate(tiles):
                    out_ref[pl.ds(base + i * SUB, SUB), lanes] = totals[i][t]
            return carry

        lax.fori_loop(0, rows // (SUB * BLOCKS), step, 0)


def correlate(grad_ref, ids_ref, ids, copies, rows, first, out_ref):
    steps = range(KERNEL // SUB)
    for tiles in lane_groups():
        for low in range(SUB):
            def step(j, sums, tiles=tiles, low=low):
                base = pl.multiple_of(j * SUB * BLOCKS, SUB * BLOCKS)
                reads = range(len(steps) + BLOCKS - 1)
                own = [ids_ref[pl.ds(base + i * SUB + first + HALF, SUB), :] for i in range(BLOCKS)]
                near = [ids[low, pl.ds(base + i * SUB + first, SUB), :] for i in reads]
                keep = {(a, i): near[a + i] == own[i] for a in steps for i in range(BLOCKS)}
                out = list(sums)
                for t, lanes in enumerate(tiles):
                    value = [copies[low, pl.ds(base + i * SUB + first, SUB), lanes] for i in reads]
                    grads = [grad_ref[pl.ds(base + i * SUB, SUB), lanes] for i in range(BLOCKS)]
                    for a in steps:
                        at = t * len(steps) + a
                        for i in range(BLOCKS):
                            out[at] = out[at] + jnp.where(keep[a, i], value[a + i], 0.0) * grads[i]
                return tuple(out)

            start = tuple(jnp.zeros((SUB, LANES), F32) for _ in range(len(steps) * len(tiles)))
            sums = lax.fori_loop(0, rows // (SUB * BLOCKS), step, start)
            for t, lanes in enumerate(tiles):
                for a in steps:
                    total = jnp.sum(sums[t * len(steps) + a], axis=0, keepdims=True)
                    out_ref[pl.ds(a * SUB + low, 1), lanes] = total


def prepare(low_ref, mid_ref, high_ref, ids_ref, copies, ids):
    @pl.when(pl.program_id(0) == 0)
    def _():
        shift_copies(ids_ref[...], ids)

    parts = [low_ref[...][: 2 * HALF], mid_ref[...], high_ref[...][: 2 * HALF]]
    shift_copies(jnp.concatenate([p.astype(F32) for p in parts]), copies)


def conv_kernel(low_ref, mid_ref, high_ref, ids_ref, taps_ref, conv_ref, stats_ref, sent_ref, copies, ids):
    rows = conv_ref.shape[0]
    prepare(low_ref, mid_ref, high_ref, ids_ref, copies, ids)
    convolve(ids_ref, ids, copies, taps_ref, conv_ref, rows, HALF, lambda o: o, 0)
    inner = conv_ref[HALF : rows - HALF, :]
    mean = jnp.sum(inner, axis=0, keepdims=True) / inner.shape[0]
    stats = jnp.concatenate([mean, jnp.sum(jnp.square(inner - mean), axis=0, keepdims=True)])
    stats_ref[...] = stats
    sent_ref[...] = jnp.broadcast_to(stats[None], sent_ref.shape)


def moments_kernel(
    low_ref, mid_ref, high_ref, ids_ref, conv_ref, stats_ref, out_ref, copies, ids, centred
):
    rows = conv_ref.shape[0] - 2 * HALF
    prepare(low_ref, mid_ref, high_ref, ids_ref, copies, ids)
    centred[...] = conv_ref[HALF : HALF + rows, :] - stats_ref[0:1, :]
    correlate(centred, ids_ref, ids, copies, rows, HALF, out_ref)


def act_kernel(
    count, low_ref, mid_ref, high_ref, ids_ref, conv_ref, back_ref, all_ref, own_ref, affine_ref, plain_ref,
    product_ref, swished_ref, grad_ref, sent_ref, norm_ref, copies, ids, centred, taps,
):
    rows = conv_ref.shape[0] - 2 * HALF
    prepare(low_ref, mid_ref, high_ref, ids_ref, copies, ids)
    merge = all_ref.shape[0]
    means = [all_ref[i, 0:1, :] for i in range(merge)]
    mean = sum(means) / merge
    spread = sum(jnp.square(m - mean) for m in means)
    var = (sum(all_ref[i, 1:2, :] for i in range(merge)) + count * spread) / (count * merge)
    inverse = lax.rsqrt(var + EPSILON)
    norm_ref[...] = jnp.concatenate([mean, inverse])
    normed = (conv_ref[...] - mean) * inverse
    act = affine_ref[0:1, :] * normed + affine_ref[1:2, :]
    gate = jax.nn.sigmoid(act)
    grad = back_ref[...] * gate * (1.0 + act * (1.0 - gate))
    grad_ref[...] = grad
    swished_ref[...] = (act * gate)[HALF : HALF + rows].astype(jnp.bfloat16)
    inner, inner_normed = grad[HALF : HALF + rows], normed[HALF : HALF + rows]
    sums = jnp.concatenate(
        [jnp.sum(inner, axis=0, keepdims=True), jnp.sum(inner * inner_normed, axis=0, keepdims=True)]
    )
    centred[...] = inner
    correlate(centred, ids_ref, ids, copies, rows, HALF, taps)
    plain = plain_ref[...]
    product = inverse * (product_ref[...] + (own_ref[0:1, :] - mean) * plain)
    chips = sent_ref.shape[0]
    each = KERNEL // chips
    for i in range(chips):
        at = slice(i * each, i * each + each)
        sent_ref[i] = jnp.concatenate([taps[at, :], plain[at], product[at], sums])


def tap_kernel(total_rows, all_ref, norm_ref, affine_ref, _, out_ref, sums_ref):
    parts = sum(all_ref[i] for i in range(all_ref.shape[0]))
    each = (parts.shape[0] - 2) // 3
    sums = parts[3 * each :]
    sums_ref[...] = sums
    scale = affine_ref[0:1, :] * norm_ref[1:2, :]
    shift, slope = sums[0:1] / total_rows, sums[1:2] / total_rows
    rest = scale * (parts[:each] - shift * parts[each : 2 * each] - slope * parts[2 * each : 3 * each])
    half = rest.shape[1] // 2
    rows = []
    for _ in range(3):
        term = rest.astype(jnp.bfloat16).astype(F32)
        for r in range(each):
            rows += [term[r : r + 1, :half], term[r : r + 1, half:]]
        rest = rest - term
    rows.append(jnp.zeros((out_ref.shape[1] - len(rows), half), F32))
    rows = jnp.concatenate(rows).astype(jnp.bfloat16)
    for i in range(out_ref.shape[0]):
        out_ref[i] = rows


def weight_kernel(own_ref, other_ref, own_grad_ref, other_grad_ref, out_ref):
    over = (((0,), (0,)), ((), ()))
    part = lax.dot_general(own_ref[...], own_grad_ref[...], over, preferred_element_type=F32)
    part = part + lax.dot_general(other_ref[...], other_grad_ref[...], over, preferred_element_type=F32)
    part = part.astype(jnp.bfloat16)
    each = part.shape[0] // out_ref.shape[0]
    for i in range(out_ref.shape[0]):
        out_ref[i, 0:each, :] = part[i * each : (i + 1) * each]


def collect_kernel(all_ref, out_ref, taps_ref):
    chips, height, _ = all_ref.shape
    rows = out_ref.shape[0] * out_ref.shape[1]
    total = sum(all_ref[i, 0:rows, :].astype(F32) for i in range(chips))
    each = out_ref.shape[1]
    for i in range(out_ref.shape[0]):
        out_ref[i] = total[i * each : (i + 1) * each]
    used = KERNEL // chips * 2
    for i in range(chips):
        terms = all_ref[i, rows:height, :].astype(F32)
        taps_ref[i] = terms[:used] + terms[used : 2 * used] + terms[2 * used : 3 * used]


def frame_kernel(
    total_rows, ids_ref, conv_ref, grad_ref, norm_ref, sums_ref, affine_ref, taps_ref, out_ref, copies, ids, result
):
    rows = out_ref.shape[0]

    @pl.when(pl.program_id(0) == 0)
    def _():
        shift_copies(ids_ref[...], ids)

    mean, inverse = norm_ref[0:1, :], norm_ref[1:2, :]
    scale = affine_ref[0:1, :] * inverse
    shift, slope = sums_ref[0:1, :] / total_rows, sums_ref[1:2, :] / total_rows
    normed = (conv_ref[...] - mean) * inverse
    grad = scale * (grad_ref[...] - shift - normed * slope)
    for b in range(SUB):
        count = rows + 2 * HALF - (SUB if b else 0)
        copies[b, 0:count, :] = grad[b : b + count]

    convolve(
        ids_ref, ids, copies, taps_ref, result, rows, 2 * HALF, lambda o: KERNEL - o, HALF
    )
    out_ref[...] = result[...].astype(jnp.bfloat16)


PARAMS = pltpu.CompilerParams(vmem_limit_bytes=48 * 1024 * 1024)


def cut(shape, width):
    lead = (0,) * (len(shape) - 1)
    if shape[-1] != width:
        return pl.BlockSpec(shape, lambda i: lead + (0,))
    return pl.BlockSpec(shape[:-1] + (TILE,), lambda i: lead + (i,))


def call(kernel, width, ins, outs, scratch, weight=1):
    return pl.pallas_call(
        kernel,
        grid=(width // TILE,),
        in_specs=[cut(a.shape, width) for a in ins],
        out_specs=[cut(shape, width) for shape, _ in outs],
        out_shape=[jax.ShapeDtypeStruct(shape, kind) for shape, kind in outs],
        scratch_shapes=scratch,
        compiler_params=PARAMS,
        cost_estimate=pl.CostEstimate(
            flops=weight * 192 * KERNEL * width * 4, bytes_accessed=4 * 224 * width * 4, transcendentals=0
        ),
    )(*ins)


def local(frame_counts, glu_out, tap_weight, bn_gain, bn_shift, proj_weight, out_grad):
    inputs = glu_out[0]
    grads_in = out_grad[0]
    frames, width = inputs.shape
    half_width = width // 2
    devices = lax.axis_size(SEQ)
    chips, column = lax.axis_size(PLANE), lax.axis_size(COLUMN)
    total_rows = frames * chips * column
    core = lax.axis_index("c")
    rows = frames + 2 * HALF
    reach = frames + 4 * HALF - SUB
    bf16 = jnp.bfloat16

    up = jnp.concatenate([inputs[-2 * HALF :], grads_in[-HALF:]])
    down = jnp.concatenate([inputs[: 2 * HALF], grads_in[:HALF]])
    low, high = shifted(up, SEQ, 1), shifted(down, SEQ, -1)
    grads_wide = jnp.concatenate([low[2 * HALF :], grads_in, high[2 * HALF :]])

    mine = lax.dynamic_slice_in_dim(grads_in, core * half_width, half_width, 1)
    other = lax.dynamic_slice_in_dim(grads_in, (1 - core) * half_width, half_width, 1)
    other = rotated(other, "c", 1)

    first = lax.axis_index(SEQ) * frames - 2 * HALF
    positions = first + jnp.arange(frames + 4 * HALF, dtype=jnp.int32)
    segments = segment_ids(frame_counts[0], positions, frames * devices)
    segments = jnp.broadcast_to(segments[:, None], (frames + 4 * HALF, LANES))
    affine = jnp.stack([bn_gain, bn_shift])
    value_copies = pltpu.VMEM((SUB, reach, TILE), F32)
    id_copies = pltpu.VMEM((SUB, reach, LANES), jnp.int32)
    column_rows = pltpu.VMEM((frames, TILE), F32)

    conv, own_stats, sent = call(
        conv_kernel, width, [low, inputs, high, segments, tap_weight],
        [((rows, width), F32), ((2, width), F32), ((chips, 2, width), F32)],
        [value_copies, id_copies],
    )
    back = lax.dot_general(
        grads_wide, proj_weight, (((1,), (1,)), ((), ())), preferred_element_type=F32
    )
    sent, back = lax.optimization_barrier((exchanged(sent, PLANE), back))
    stats, conv = lax.optimization_barrier((merged(sent, frames), conv))
    (product,) = call(
        moments_kernel, width, [low, inputs, high, segments, conv, own_stats], [((KERNEL, width), F32)],
        [value_copies, id_copies, column_rows],
    )
    wide = jnp.concatenate([low[: 2 * HALF], inputs, high[: 2 * HALF]])
    plain = jnp.dot(
        window_mask(frame_counts[0], first, frames, frames * devices), wide, preferred_element_type=F32
    )
    stats = gathered(stats, COLUMN)

    each = KERNEL // chips
    swished, act_grad, sent, norm = call(
        functools.partial(act_kernel, frames * chips), width,
        [low, inputs, high, segments, conv, back, stats, own_stats, affine, plain, product],
        [((frames, width), bf16), ((rows, width), F32), ((chips, 3 * each + 2, width), F32), ((2, width), F32)],
        [value_copies, id_copies, column_rows, pltpu.VMEM((KERNEL, TILE), F32)],
    )
    sent = exchanged(sent, PLANE)

    share = width // chips
    height = share + 16 * -(-6 * each // 16)
    part = pl.pallas_call(
        weight_kernel,
        grid=(4,),
        in_specs=[pl.BlockSpec((frames, width // 4), lambda i: (0, i))] * 2
        + [pl.BlockSpec((frames, half_width), lambda i: (0, 0))] * 2,
        out_specs=pl.BlockSpec((chips // 4, height, half_width), lambda i: (i, 0, 0)),
        out_shape=jax.ShapeDtypeStruct((chips, height, half_width), bf16),
        compiler_params=PARAMS,
        cost_estimate=pl.CostEstimate(
            flops=4 * frames * width * half_width, bytes_accessed=6 * width * half_width, transcendentals=0
        ),
    )(swished, rotated(swished, "c", 1), mine, other)
    block = jnp.dot(swished, proj_weight, preferred_element_type=F32).astype(bf16)
    sent, part, block = lax.optimization_barrier((sent, part, block))
    sent = gathered(jnp.sum(sent, axis=0), COLUMN)

    at = share // (height - share)
    part, sums = pl.pallas_call(
        functools.partial(tap_kernel, total_rows),
        grid=(1,),
        in_specs=[cut(sent.shape, 0), cut(norm.shape, 0), cut(affine.shape, 0), pl.BlockSpec(memory_space=pl.ANY)],
        out_specs=[
            pl.BlockSpec((chips, height - share, half_width), lambda i: (0, at, 0)),
            cut((2, width), 0),
        ],
        out_shape=[jax.ShapeDtypeStruct(part.shape, bf16), jax.ShapeDtypeStruct((2, width), F32)],
        input_output_aliases={3: 0},
        compiler_params=PARAMS,
    )(sent, norm, affine, part)
    part = exchanged(part, PLANE)

    (frame_grad,) = call(
        functools.partial(frame_kernel, total_rows), width,
        [segments, conv, act_grad, norm, sums, affine, tap_weight], [((frames, width), bf16)],
        [value_copies, id_copies, column_rows],
    )
    part, frame_grad = lax.optimization_barrier((part, frame_grad))
    part, tap_grad = pl.pallas_call(
        collect_kernel,
        grid=(1,),
        in_specs=[cut(part.shape, 0)],
        out_specs=[cut((column, share // column, half_width), 0), cut((chips, 2 * each, half_width), 0)],
        out_shape=[
            jax.ShapeDtypeStruct((column, share // column, half_width), F32),
            jax.ShapeDtypeStruct((chips, 2 * each, half_width), F32),
        ],
        compiler_params=PARAMS,
    )(part)
    part = exchanged(part, COLUMN)
    part = jnp.sum(part.reshape((2, column // 2) + part.shape[1:]), axis=1)
    proj_grad = jnp.concatenate([part[0], part[1]], axis=1)
    tap_grad = tap_grad.reshape(KERNEL, width)
    return (block[None], frame_grad[None], tap_grad, sums[1], sums[0], proj_grad)


def solution(mesh):
    grid = Mesh(mesh.devices.reshape(4, 4, 2, -1), ("x", "y", "c", "z"))
    wide = P("z", SEQ, None)
    return jax.shard_map(
        local,
        mesh=grid,
        in_specs=(P("z", None), wide, P(), P(), P(), P(), wide),
        out_specs=(wide, wide, P(), P(), P(), P(("x", "y", "c", "z"), None)),
        check_vma=False,
    )
```

```python
import functools

import jax
import jax.numpy as jnp
from jax import lax
from jax.experimental import pallas as pl
from jax.experimental.pallas import tpu as pltpu
from jax.sharding import Mesh, PartitionSpec as P

HALF = 16
KERNEL = 2 * HALF
EPSILON = 1e-05
SEQ = ("x", "y", "c")
PLANE = ("x", "y")
COLUMN = ("c", "z")
LANES = 128
TILE = 512
SUB = 8
BLOCKS = 4
GROUP = 4
F32 = jnp.float32


def shifted(value, axes, step):
    count = lax.axis_size(axes)
    pairs = [(i, i + step) for i in range(count) if 0 <= i + step < count]
    return lax.ppermute(value, axes, pairs)


def rotated(value, axis, step):
    count = lax.axis_size(axis)
    return lax.ppermute(value, axis, [(i, (i + step) % count) for i in range(count)])


def exchanged(blocks, axes):
    return lax.all_to_all(blocks, axes, 0, 0, tiled=True)


def gathered(value, axes):
    count = lax.axis_size(axes)
    return exchanged(jnp.broadcast_to(value[None], (count,) + value.shape), axes)


def merged(stats, count):
    means, squares = stats[:, 0], stats[:, 1]
    mean = jnp.mean(means, axis=0)
    spread = jnp.sum(jnp.square(means - mean), axis=0)
    return jnp.stack([mean, jnp.sum(squares, axis=0) + count * spread])


def segment_ids(counts, positions, frames):
    ends = jnp.cumsum(counts)
    found = jnp.sum((positions[:, None] >= ends[None, :]).astype(jnp.int32), axis=1)
    return jnp.where((positions >= 0) & (positions < frames), found, -1)


def window_mask(counts, first, frames, limit):
    row = lax.broadcasted_iota(jnp.int32, (KERNEL, frames + 4 * HALF), 1)
    owner = row + HALF - lax.broadcasted_iota(jnp.int32, row.shape, 0)
    ends = jnp.cumsum(counts)[:, None, None]
    same = jnp.all((first + row >= ends) == (first + owner >= ends), axis=0)
    inside = (owner >= 2 * HALF) & (owner < 2 * HALF + frames)
    valid = (first + row >= 0) & (first + row < limit)
    return (same & inside & valid).astype(jnp.bfloat16)


def shift_copies(source, copies):
    rows = copies.shape[1]
    for b in range(SUB):
        copies[b] = source[b : b + rows]


def lane_groups():
    tiles = [pl.ds(t * LANES, LANES) for t in range(TILE // LANES)]
    return [tiles[t : t + GROUP] for t in range(0, len(tiles), GROUP)]


def convolve(ids_ref, ids, copies, taps_ref, out_ref, rows, centre, tap_of, id_shift):
    offsets = [o for o in range(KERNEL + 1) if 0 <= tap_of(o) < KERNEL]
    for tiles in lane_groups():
        def step(j, carry, tiles=tiles):
            base = pl.multiple_of(j * SUB * BLOCKS, SUB * BLOCKS)
            own = [ids_ref[pl.ds(base + i * SUB + centre, SUB), :] for i in range(BLOCKS)]
            totals = [[jnp.zeros((SUB, LANES), F32) for _ in tiles] for _ in range(BLOCKS)]
            for low in range(SUB):
                steps = [o // SUB for o in offsets if o % SUB == low]
                reads = range(min(steps), max(steps) + BLOCKS)
                near = {i: ids[low, pl.ds(base + i * SUB + id_shift, SUB), :] for i in reads}
                keep = {(a, i): near[a + i] == own[i] for a in steps for i in range(BLOCKS)}
                for t, lanes in enumerate(tiles):
                    value = {i: copies[low, pl.ds(base + i * SUB, SUB), lanes] for i in reads}
                    for a in steps:
                        tap = taps_ref[pl.ds(tap_of(a * SUB + low), 1), lanes]
                        for i in range(BLOCKS):
                            term = jnp.where(keep[a, i], value[a + i], 0.0)
                            totals[i][t] = totals[i][t] + tap * term
            for i in range(BLOCKS):
                for t, lanes in enumerate(tiles):
                    out_ref[pl.ds(base + i * SUB, SUB), lanes] = totals[i][t]
            return carry

        lax.fori_loop(0, rows // (SUB * BLOCKS), step, 0)


def correlate(grad_ref, ids_ref, ids, copies, rows, first, out_ref):
    steps = range(KERNEL // SUB)
    for tiles in lane_groups():
        for low in range(SUB):
            def step(j, sums, tiles=tiles, low=low):
                base = pl.multiple_of(j * SUB * BLOCKS, SUB * BLOCKS)
                reads = range(len(steps) + BLOCKS - 1)
                own = [ids_ref[pl.ds(base + i * SUB + first + HALF, SUB), :] for i in range(BLOCKS)]
                near = [ids[low, pl.ds(base + i * SUB + first, SUB), :] for i in reads]
                keep = {(a, i): near[a + i] == own[i] for a in steps for i in range(BLOCKS)}
                out = list(sums)
                for t, lanes in enumerate(tiles):
                    value = [copies[low, pl.ds(base + i * SUB + first, SUB), lanes] for i in reads]
                    grads = [grad_ref[pl.ds(base + i * SUB, SUB), lanes] for i in range(BLOCKS)]
                    for a in steps:
                        at = t * len(steps) + a
                        for i in range(BLOCKS):
                            out[at] = out[at] + jnp.where(keep[a, i], value[a + i], 0.0) * grads[i]
                return tuple(out)

            start = tuple(jnp.zeros((SUB, LANES), F32) for _ in range(len(steps) * len(tiles)))
            sums = lax.fori_loop(0, rows // (SUB * BLOCKS), step, start)
            for t, lanes in enumerate(tiles):
                for a in steps:
                    total = jnp.sum(sums[t * len(steps) + a], axis=0, keepdims=True)
                    out_ref[pl.ds(a * SUB + low, 1), lanes] = total


def prepare(low_ref, mid_ref, high_ref, ids_ref, copies, ids):
    @pl.when(pl.program_id(0) == 0)
    def _():
        shift_copies(ids_ref[...], ids)

    parts = [low_ref[...][: 2 * HALF], mid_ref[...], high_ref[...][: 2 * HALF]]
    shift_copies(jnp.concatenate([p.astype(F32) for p in parts]), copies)


def conv_kernel(low_ref, mid_ref, high_ref, ids_ref, taps_ref, conv_ref, stats_ref, sent_ref, copies, ids):
    rows = conv_ref.shape[0]
    prepare(low_ref, mid_ref, high_ref, ids_ref, copies, ids)
    convolve(ids_ref, ids, copies, taps_ref, conv_ref, rows, HALF, lambda o: o, 0)
    inner = conv_ref[HALF : rows - HALF, :]
    mean = jnp.sum(inner, axis=0, keepdims=True) / inner.shape[0]
    stats = jnp.concatenate([mean, jnp.sum(jnp.square(inner - mean), axis=0, keepdims=True)])
    stats_ref[...] = stats
    sent_ref[...] = jnp.broadcast_to(stats[None], sent_ref.shape)


def moments_kernel(
    low_ref, mid_ref, high_ref, ids_ref, conv_ref, stats_ref, out_ref, copies, ids, centred
):
    rows = conv_ref.shape[0] - 2 * HALF
    prepare(low_ref, mid_ref, high_ref, ids_ref, copies, ids)
    centred[...] = conv_ref[HALF : HALF + rows, :] - stats_ref[0:1, :]
    correlate(centred, ids_ref, ids, copies, rows, HALF, out_ref)


def act_kernel(
    count, core_ref, low_ref, mid_ref, high_ref, ids_ref, conv_ref, back_ref, all_ref, own_ref, affine_ref,
    plain_ref, product_ref, swished_ref, grad_ref, kept_ref, given_ref, norm_ref, copies, ids, centred, taps,
):
    rows = conv_ref.shape[0] - 2 * HALF
    prepare(low_ref, mid_ref, high_ref, ids_ref, copies, ids)
    merge = all_ref.shape[0]
    means = [all_ref[i, 0:1, :] for i in range(merge)]
    mean = sum(means) / merge
    spread = sum(jnp.square(m - mean) for m in means)
    var = (sum(all_ref[i, 1:2, :] for i in range(merge)) + count * spread) / (count * merge)
    inverse = lax.rsqrt(var + EPSILON)
    norm_ref[...] = jnp.concatenate([mean, inverse])
    normed = (conv_ref[...] - mean) * inverse
    act = affine_ref[0:1, :] * normed + affine_ref[1:2, :]
    gate = jax.nn.sigmoid(act)
    grad = back_ref[...] * gate * (1.0 + act * (1.0 - gate))
    grad_ref[...] = grad
    swished_ref[...] = (act * gate)[HALF : HALF + rows].astype(jnp.bfloat16)
    inner, inner_normed = grad[HALF : HALF + rows], normed[HALF : HALF + rows]
    sums = [jnp.sum(inner, axis=0, keepdims=True), jnp.sum(inner * inner_normed, axis=0, keepdims=True)]
    centred[...] = inner
    correlate(centred, ids_ref, ids, copies, rows, HALF, taps)
    plain = plain_ref[...]
    product = inverse * (product_ref[...] + (own_ref[0:1, :] - mean) * plain)
    chips = kept_ref.shape[0]
    first = core_ref[0] == 0
    for i in range(chips):
        low, high = (
            jnp.concatenate([v[at : at + 1] for v in (taps, plain, product)] + [sums[at // chips]])
            for at in (i, chips + i)
        )
        kept_ref[i] = jnp.where(first, low, high)
        given_ref[i] = jnp.where(first, high, low)


def tap_kernel(total_rows, parts_ref, sums_ref, norm_ref, affine_ref, _, out_ref):
    scale = affine_ref[0:1, :] * norm_ref[1:2, :]
    shift, slope = sums_ref[0:1, :] / total_rows, sums_ref[1:2, :] / total_rows
    rest = scale * (parts_ref[0:1, :] - shift * parts_ref[1:2, :] - slope * parts_ref[2:3, :])
    half = rest.shape[1] // 2
    rows = []
    for _ in range(3):
        term = rest.astype(jnp.bfloat16).astype(F32)
        rows += [term[:, :half], term[:, half:]]
        rest = rest - term
    rows.append(jnp.zeros((out_ref.shape[1] - len(rows), half), F32))
    rows = jnp.concatenate(rows).astype(jnp.bfloat16)
    for i in range(out_ref.shape[0]):
        out_ref[i] = rows


def weight_kernel(own_ref, other_ref, own_grad_ref, other_grad_ref, out_ref):
    over = (((0,), (0,)), ((), ()))
    part = lax.dot_general(own_ref[...], own_grad_ref[...], over, preferred_element_type=F32)
    part = part + lax.dot_general(other_ref[...], other_grad_ref[...], over, preferred_element_type=F32)
    part = part.astype(jnp.bfloat16)
    each = part.shape[0] // out_ref.shape[0]
    for i in range(out_ref.shape[0]):
        out_ref[i, 0:each, :] = part[i * each : (i + 1) * each]


def collect_kernel(all_ref, out_ref, taps_ref):
    chips, height, _ = all_ref.shape
    rows = out_ref.shape[0] * out_ref.shape[1]
    total = sum(all_ref[i, 0:rows, :].astype(F32) for i in range(chips))
    each = out_ref.shape[1]
    for i in range(out_ref.shape[0]):
        out_ref[i] = total[i * each : (i + 1) * each]
    half = out_ref.shape[2]
    for i in range(chips):
        terms = all_ref[i, rows:height, :].astype(F32)
        terms = terms[0:2] + terms[2:4] + terms[4:6]
        taps_ref[i : i + 1, :half] = terms[0:1]
        taps_ref[i : i + 1, half:] = terms[1:2]


def frame_kernel(
    total_rows, ids_ref, conv_ref, grad_ref, norm_ref, sums_ref, affine_ref, taps_ref, out_ref, copies, ids, result
):
    rows = out_ref.shape[0]

    @pl.when(pl.program_id(0) == 0)
    def _():
        shift_copies(ids_ref[...], ids)

    mean, inverse = norm_ref[0:1, :], norm_ref[1:2, :]
    scale = affine_ref[0:1, :] * inverse
    shift, slope = sums_ref[0:1, :] / total_rows, sums_ref[1:2, :] / total_rows
    normed = (conv_ref[...] - mean) * inverse
    grad = scale * (grad_ref[...] - shift - normed * slope)
    for b in range(SUB):
        count = rows + 2 * HALF - (SUB if b else 0)
        copies[b, 0:count, :] = grad[b : b + count]

    convolve(
        ids_ref, ids, copies, taps_ref, result, rows, 2 * HALF, lambda o: KERNEL - o, HALF
    )
    out_ref[...] = result[...].astype(jnp.bfloat16)


PARAMS = pltpu.CompilerParams(vmem_limit_bytes=48 * 1024 * 1024)


def cut(shape, width):
    lead = (0,) * (len(shape) - 1)
    if shape == (1,):
        return pl.BlockSpec(memory_space=pltpu.SMEM)
    if shape[-1] != width:
        return pl.BlockSpec(shape, lambda i: lead + (0,))
    return pl.BlockSpec(shape[:-1] + (TILE,), lambda i: lead + (i,))


def call(kernel, width, ins, outs, scratch, weight=1):
    return pl.pallas_call(
        kernel,
        grid=(width // TILE,),
        in_specs=[cut(a.shape, width) for a in ins],
        out_specs=[cut(shape, width) for shape, _ in outs],
        out_shape=[jax.ShapeDtypeStruct(shape, kind) for shape, kind in outs],
        scratch_shapes=scratch,
        compiler_params=PARAMS,
        cost_estimate=pl.CostEstimate(
            flops=weight * 192 * KERNEL * width * 4, bytes_accessed=4 * 224 * width * 4, transcendentals=0
        ),
    )(*ins)


def local(frame_counts, glu_out, tap_weight, bn_gain, bn_shift, proj_weight, out_grad):
    inputs = glu_out[0]
    grads_in = out_grad[0]
    frames, width = inputs.shape
    half_width = width // 2
    devices = lax.axis_size(SEQ)
    chips, column = lax.axis_size(PLANE), lax.axis_size(COLUMN)
    total_rows = frames * chips * column
    core = lax.axis_index("c")
    rows = frames + 2 * HALF
    reach = frames + 4 * HALF - SUB
    bf16 = jnp.bfloat16

    up = jnp.concatenate([inputs[-2 * HALF :], grads_in[-HALF:]])
    down = jnp.concatenate([inputs[: 2 * HALF], grads_in[:HALF]])
    low, high = shifted(up, SEQ, 1), shifted(down, SEQ, -1)
    grads_wide = jnp.concatenate([low[2 * HALF :], grads_in, high[2 * HALF :]])

    first = lax.axis_index(SEQ) * frames - 2 * HALF
    positions = first + jnp.arange(frames + 4 * HALF, dtype=jnp.int32)
    segments = segment_ids(frame_counts[0], positions, frames * devices)
    segments = jnp.broadcast_to(segments[:, None], (frames + 4 * HALF, LANES))
    affine = jnp.stack([bn_gain, bn_shift])
    value_copies = pltpu.VMEM((SUB, reach, TILE), F32)
    id_copies = pltpu.VMEM((SUB, reach, LANES), jnp.int32)
    column_rows = pltpu.VMEM((frames, TILE), F32)

    conv, own_stats, sent = call(
        conv_kernel, width, [low, inputs, high, segments, tap_weight],
        [((rows, width), F32), ((2, width), F32), ((chips, 2, width), F32)],
        [value_copies, id_copies],
    )
    back = lax.dot_general(
        grads_wide, proj_weight, (((1,), (1,)), ((), ())), preferred_element_type=F32
    )
    sent, back, grads_in = lax.optimization_barrier((exchanged(sent, PLANE), back, grads_in))
    mine = lax.dynamic_slice_in_dim(grads_in, core * half_width, half_width, 1)
    other = lax.dynamic_slice_in_dim(grads_in, (1 - core) * half_width, half_width, 1)
    other = rotated(other, "c", 1)
    stats, conv = lax.optimization_barrier((merged(sent, frames), conv))
    (product,) = call(
        moments_kernel, width, [low, inputs, high, segments, conv, own_stats], [((KERNEL, width), F32)],
        [value_copies, id_copies, column_rows],
    )
    wide = jnp.concatenate([low[: 2 * HALF], inputs, high[: 2 * HALF]])
    plain = jnp.dot(
        window_mask(frame_counts[0], first, frames, frames * devices), wide, preferred_element_type=F32
    )
    stats = gathered(stats, COLUMN)

    swished, act_grad, kept, given, norm = call(
        functools.partial(act_kernel, frames * chips), width,
        [core.reshape(1), low, inputs, high, segments, conv, back, stats, own_stats, affine, plain, product],
        [((frames, width), bf16), ((rows, width), F32), ((chips, 4, width), F32), ((chips, 4, width), F32),
         ((2, width), F32)],
        [value_copies, id_copies, column_rows, pltpu.VMEM((KERNEL, TILE), F32)],
    )
    sent, swished = lax.optimization_barrier((kept + rotated(given, "c", 1), swished))
    sent = exchanged(sent, PLANE)

    share = width // chips
    height = share + 16
    part = pl.pallas_call(
        weight_kernel,
        grid=(4,),
        in_specs=[pl.BlockSpec((frames, width // 4), lambda i: (0, i))] * 2
        + [pl.BlockSpec((frames, half_width), lambda i: (0, 0))] * 2,
        out_specs=pl.BlockSpec((chips // 4, height, half_width), lambda i: (i, 0, 0)),
        out_shape=jax.ShapeDtypeStruct((chips, height, half_width), bf16),
        compiler_params=PARAMS,
        cost_estimate=pl.CostEstimate(
            flops=4 * frames * width * half_width, bytes_accessed=6 * width * half_width, transcendentals=0
        ),
    )(swished, rotated(swished, "c", 1), mine, other)
    block = jnp.dot(swished, proj_weight, preferred_element_type=F32).astype(bf16)
    sent, part = lax.optimization_barrier((sent, part))
    sent = jnp.sum(gathered(jnp.sum(sent, axis=0), "z"), axis=0)
    own_sum = sent[3:]
    sums = jnp.concatenate([own_sum, rotated(own_sum, "c", 1)])
    sums = jnp.where(core == 0, sums, sums[::-1])

    at = share // (height - share)
    part = pl.pallas_call(
        functools.partial(tap_kernel, total_rows),
        grid=(1,),
        in_specs=[cut(a.shape, 0) for a in (sent, sums, norm, affine)] + [pl.BlockSpec(memory_space=pl.ANY)],
        out_specs=pl.BlockSpec((chips, height - share, half_width), lambda i: (0, at, 0)),
        out_shape=jax.ShapeDtypeStruct(part.shape, bf16),
        input_output_aliases={4: 0},
        compiler_params=PARAMS,
    )(sent, sums, norm, affine, part)
    part = exchanged(part, PLANE)

    (frame_grad,) = call(
        functools.partial(frame_kernel, total_rows), width,
        [segments, conv, act_grad, norm, sums, affine, tap_weight], [((frames, width), bf16)],
        [value_copies, id_copies, column_rows],
    )
    part, frame_grad, block = lax.optimization_barrier((part, frame_grad, block))
    part, tap_grad = pl.pallas_call(
        collect_kernel,
        grid=(1,),
        in_specs=[cut(part.shape, 0)],
        out_specs=[cut((column, share // column, half_width), 0), cut((chips, width), 0)],
        out_shape=[
            jax.ShapeDtypeStruct((column, share // column, half_width), F32),
            jax.ShapeDtypeStruct((chips, width), F32),
        ],
        compiler_params=PARAMS,
    )(part)
    other_taps = rotated(tap_grad, "c", 1)
    part = exchanged(part, COLUMN)
    part = jnp.sum(part.reshape((2, column // 2) + part.shape[1:]), axis=1)
    proj_grad = jnp.concatenate([part[0], part[1]], axis=1)
    tap_grad = jnp.where(
        core == 0, jnp.concatenate([tap_grad, other_taps]), jnp.concatenate([other_taps, tap_grad])
    )
    return (block[None], frame_grad[None], tap_grad, sums[1], sums[0], proj_grad)


def solution(mesh):
    grid = Mesh(mesh.devices.reshape(4, 4, 2, -1), ("x", "y", "c", "z"))
    wide = P("z", SEQ, None)
    return jax.shard_map(
        local,
        mesh=grid,
        in_specs=(P("z", None), wide, P(), P(), P(), P(), wide),
        out_specs=(wide, wide, P(), P(), P(), P(("x", "y", "c", "z"), None)),
        check_vma=False,
    )
```

```python
import functools

import jax
import jax.numpy as jnp
from jax import lax
from jax.experimental import pallas as pl
from jax.experimental.pallas import tpu as pltpu
from jax.sharding import Mesh, PartitionSpec as P

HALF = 16
KERNEL = 2 * HALF
EPSILON = 1e-05
SEQ = ("x", "y", "c")
PLANE = ("x", "y")
COLUMN = ("c", "z")
LANES = 128
TILE = 512
SUB = 8
BLOCKS = 4
GROUP = 4
F32 = jnp.float32


def shifted(value, axes, step):
    count = lax.axis_size(axes)
    pairs = [(i, i + step) for i in range(count) if 0 <= i + step < count]
    return lax.ppermute(value, axes, pairs)


def rotated(value, axis, step):
    count = lax.axis_size(axis)
    return lax.ppermute(value, axis, [(i, (i + step) % count) for i in range(count)])


def crossed(value, axis, bit):
    count = lax.axis_size(axis)
    return lax.ppermute(value, axis, [(i, i ^ bit) for i in range(count)])


def doubled(value, axis, bit):
    other = crossed(value, axis, bit)
    upper = (lax.axis_index(axis) & bit) != 0
    first, second = jnp.where(upper, other, value), jnp.where(upper, value, other)
    return jnp.concatenate([first, second])


def exchanged(blocks, axes):
    return lax.all_to_all(blocks, axes, 0, 0, tiled=True)


def gathered(value, axes):
    count = lax.axis_size(axes)
    return exchanged(jnp.broadcast_to(value[None], (count,) + value.shape), axes)


def merged(stats, count):
    means, squares = stats[:, 0], stats[:, 1]
    mean = jnp.mean(means, axis=0)
    spread = jnp.sum(jnp.square(means - mean), axis=0)
    return jnp.stack([mean, jnp.sum(squares, axis=0) + count * spread])


def segment_ids(counts, positions, frames):
    ends = jnp.cumsum(counts)
    found = jnp.sum((positions[:, None] >= ends[None, :]).astype(jnp.int32), axis=1)
    return jnp.where((positions >= 0) & (positions < frames), found, -1)


def window_mask(counts, first, frames, limit):
    row = lax.broadcasted_iota(jnp.int32, (KERNEL, frames + 4 * HALF), 1)
    owner = row + HALF - lax.broadcasted_iota(jnp.int32, row.shape, 0)
    ends = jnp.cumsum(counts)[:, None, None]
    same = jnp.all((first + row >= ends) == (first + owner >= ends), axis=0)
    inside = (owner >= 2 * HALF) & (owner < 2 * HALF + frames)
    valid = (first + row >= 0) & (first + row < limit)
    return (same & inside & valid).astype(jnp.bfloat16)


def shift_copies(source, copies):
    rows = copies.shape[1]
    for b in range(SUB):
        copies[b] = source[b : b + rows]


def lane_groups():
    tiles = [pl.ds(t * LANES, LANES) for t in range(TILE // LANES)]
    return [tiles[t : t + GROUP] for t in range(0, len(tiles), GROUP)]


def convolve(ids_ref, ids, copies, taps_ref, out_ref, rows, centre, tap_of, id_shift):
    offsets = [o for o in range(KERNEL + 1) if 0 <= tap_of(o) < KERNEL]
    for tiles in lane_groups():
        def step(j, carry, tiles=tiles):
            base = pl.multiple_of(j * SUB * BLOCKS, SUB * BLOCKS)
            own = [ids_ref[pl.ds(base + i * SUB + centre, SUB), :] for i in range(BLOCKS)]
            totals = [[jnp.zeros((SUB, LANES), F32) for _ in tiles] for _ in range(BLOCKS)]
            for low in range(SUB):
                steps = [o // SUB for o in offsets if o % SUB == low]
                reads = range(min(steps), max(steps) + BLOCKS)
                near = {i: ids[low, pl.ds(base + i * SUB + id_shift, SUB), :] for i in reads}
                keep = {(a, i): near[a + i] == own[i] for a in steps for i in range(BLOCKS)}
                for t, lanes in enumerate(tiles):
                    value = {i: copies[low, pl.ds(base + i * SUB, SUB), lanes] for i in reads}
                    for a in steps:
                        tap = taps_ref[pl.ds(tap_of(a * SUB + low), 1), lanes]
                        for i in range(BLOCKS):
                            term = jnp.where(keep[a, i], value[a + i], 0.0)
                            totals[i][t] = totals[i][t] + tap * term
            for i in range(BLOCKS):
                for t, lanes in enumerate(tiles):
                    out_ref[pl.ds(base + i * SUB, SUB), lanes] = totals[i][t]
            return carry

        lax.fori_loop(0, rows // (SUB * BLOCKS), step, 0)


def correlate(grad_ref, ids_ref, ids, copies, rows, first, out_ref):
    steps = range(KERNEL // SUB)
    for tiles in lane_groups():
        for low in range(SUB):
            def step(j, sums, tiles=tiles, low=low):
                base = pl.multiple_of(j * SUB * BLOCKS, SUB * BLOCKS)
                reads = range(len(steps) + BLOCKS - 1)
                own = [ids_ref[pl.ds(base + i * SUB + first + HALF, SUB), :] for i in range(BLOCKS)]
                near = [ids[low, pl.ds(base + i * SUB + first, SUB), :] for i in reads]
                keep = {(a, i): near[a + i] == own[i] for a in steps for i in range(BLOCKS)}
                out = list(sums)
                for t, lanes in enumerate(tiles):
                    value = [copies[low, pl.ds(base + i * SUB + first, SUB), lanes] for i in reads]
                    grads = [grad_ref[pl.ds(base + i * SUB, SUB), lanes] for i in range(BLOCKS)]
                    for a in steps:
                        at = t * len(steps) + a
                        for i in range(BLOCKS):
                            out[at] = out[at] + jnp.where(keep[a, i], value[a + i], 0.0) * grads[i]
                return tuple(out)

            start = tuple(jnp.zeros((SUB, LANES), F32) for _ in range(len(steps) * len(tiles)))
            sums = lax.fori_loop(0, rows // (SUB * BLOCKS), step, start)
            for t, lanes in enumerate(tiles):
                for a in steps:
                    total = jnp.sum(sums[t * len(steps) + a], axis=0, keepdims=True)
                    out_ref[pl.ds(a * SUB + low, 1), lanes] = total


def prepare(low_ref, mid_ref, high_ref, ids_ref, copies, ids):
    @pl.when(pl.program_id(0) == 0)
    def _():
        shift_copies(ids_ref[...], ids)

    parts = [low_ref[...][: 2 * HALF], mid_ref[...], high_ref[...][: 2 * HALF]]
    shift_copies(jnp.concatenate([p.astype(F32) for p in parts]), copies)


def conv_kernel(low_ref, mid_ref, high_ref, ids_ref, taps_ref, conv_ref, stats_ref, sent_ref, copies, ids):
    rows = conv_ref.shape[0]
    prepare(low_ref, mid_ref, high_ref, ids_ref, copies, ids)
    convolve(ids_ref, ids, copies, taps_ref, conv_ref, rows, HALF, lambda o: o, 0)
    inner = conv_ref[HALF : rows - HALF, :]
    mean = jnp.sum(inner, axis=0, keepdims=True) / inner.shape[0]
    stats = jnp.concatenate([mean, jnp.sum(jnp.square(inner - mean), axis=0, keepdims=True)])
    stats_ref[...] = stats
    sent_ref[...] = jnp.broadcast_to(stats[None], sent_ref.shape)


def moments_kernel(
    low_ref, mid_ref, high_ref, ids_ref, conv_ref, stats_ref, out_ref, copies, ids, centred
):
    rows = conv_ref.shape[0] - 2 * HALF
    prepare(low_ref, mid_ref, high_ref, ids_ref, copies, ids)
    centred[...] = conv_ref[HALF : HALF + rows, :] - stats_ref[0:1, :]
    correlate(centred, ids_ref, ids, copies, rows, HALF, out_ref)


def act_kernel(
    count, core_ref, low_ref, mid_ref, high_ref, ids_ref, conv_ref, back_ref, all_ref, own_ref, affine_ref,
    plain_ref, product_ref, swished_ref, grad_ref, kept_ref, given_ref, norm_ref, copies, ids, centred, taps,
):
    rows = conv_ref.shape[0] - 2 * HALF
    prepare(low_ref, mid_ref, high_ref, ids_ref, copies, ids)
    merge = all_ref.shape[0]
    means = [all_ref[i, 0:1, :] for i in range(merge)]
    mean = sum(means) / merge
    spread = sum(jnp.square(m - mean) for m in means)
    var = (sum(all_ref[i, 1:2, :] for i in range(merge)) + count * spread) / (count * merge)
    inverse = lax.rsqrt(var + EPSILON)
    norm_ref[...] = jnp.concatenate([mean, inverse])
    normed = (conv_ref[...] - mean) * inverse
    act = affine_ref[0:1, :] * normed + affine_ref[1:2, :]
    gate = jax.nn.sigmoid(act)
    grad = back_ref[...] * gate * (1.0 + act * (1.0 - gate))
    grad_ref[...] = grad
    swished_ref[...] = (act * gate)[HALF : HALF + rows].astype(jnp.bfloat16)
    inner, inner_normed = grad[HALF : HALF + rows], normed[HALF : HALF + rows]
    sums = [jnp.sum(inner, axis=0, keepdims=True), jnp.sum(inner * inner_normed, axis=0, keepdims=True)]
    centred[...] = inner
    correlate(centred, ids_ref, ids, copies, rows, HALF, taps)
    plain = plain_ref[...]
    product = inverse * (product_ref[...] + (own_ref[0:1, :] - mean) * plain)
    chips = kept_ref.shape[0]
    first = core_ref[0] == 0
    for i in range(chips):
        low, high = (
            jnp.concatenate([v[at : at + 1] for v in (taps, plain, product)] + [sums[at // chips]])
            for at in (i, chips + i)
        )
        kept_ref[i] = jnp.where(first, low, high)
        given_ref[i] = jnp.where(first, high, low)


def weight_kernel(own_ref, other_ref, own_grad_ref, other_grad_ref, left_ref, right_ref):
    over = (((0,), (0,)), ((), ()))
    part = lax.dot_general(own_ref[...], own_grad_ref[...], over, preferred_element_type=F32)
    part = part + lax.dot_general(other_ref[...], other_grad_ref[...], over, preferred_element_type=F32)
    part = part.astype(jnp.bfloat16)
    each, half = left_ref.shape[1:]
    for i in range(left_ref.shape[0]):
        left_ref[i] = part[i * each : (i + 1) * each, :half]
        right_ref[i, 0:each, :] = part[i * each : (i + 1) * each, half:]


def tap_kernel(total_rows, parts_ref, sums_ref, norm_ref, affine_ref, _, out_ref):
    scale = affine_ref[0:1, :] * norm_ref[1:2, :]
    shift, slope = sums_ref[0:1, :] / total_rows, sums_ref[1:2, :] / total_rows
    rest = scale * (parts_ref[0:1, :] - shift * parts_ref[1:2, :] - slope * parts_ref[2:3, :])
    height, size = out_ref.shape[1:]
    rows = []
    for _ in range(3):
        term = rest.astype(jnp.bfloat16).astype(F32)
        rows += [term[:, at : at + size] for at in range(0, rest.shape[1], size)]
        rest = rest - term
    rows.append(jnp.zeros((height - len(rows), size), F32))
    rows = jnp.concatenate(rows).astype(jnp.bfloat16)
    for i in range(out_ref.shape[0]):
        out_ref[i] = rows


def collect_kernel(left_ref, right_ref, out_ref, taps_ref):
    each = out_ref.shape[1]
    half = left_ref.shape[2]
    for all_ref, columns in ((left_ref, slice(0, half)), (right_ref, slice(half, 2 * half))):
        total = sum(all_ref[i, 0 : left_ref.shape[1], :].astype(F32) for i in range(all_ref.shape[0]))
        for i in range(out_ref.shape[0]):
            out_ref[i, :, columns] = total[i * each : (i + 1) * each]
    for i in range(right_ref.shape[0]):
        terms = right_ref[i, left_ref.shape[1] :, :].astype(F32)
        terms = terms[0:4] + terms[4:8] + terms[8:12]
        for piece in range(4):
            taps_ref[i : i + 1, piece * half : (piece + 1) * half] = terms[piece : piece + 1]


def frame_kernel(
    total_rows, ids_ref, conv_ref, grad_ref, norm_ref, sums_ref, affine_ref, taps_ref, out_ref, copies, ids, result
):
    rows = out_ref.shape[0]

    @pl.when(pl.program_id(0) == 0)
    def _():
        shift_copies(ids_ref[...], ids)

    mean, inverse = norm_ref[0:1, :], norm_ref[1:2, :]
    scale = affine_ref[0:1, :] * inverse
    shift, slope = sums_ref[0:1, :] / total_rows, sums_ref[1:2, :] / total_rows
    normed = (conv_ref[...] - mean) * inverse
    grad = scale * (grad_ref[...] - shift - normed * slope)
    for b in range(SUB):
        count = rows + 2 * HALF - (SUB if b else 0)
        copies[b, 0:count, :] = grad[b : b + count]

    convolve(
        ids_ref, ids, copies, taps_ref, result, rows, 2 * HALF, lambda o: KERNEL - o, HALF
    )
    out_ref[...] = result[...].astype(jnp.bfloat16)


PARAMS = pltpu.CompilerParams(vmem_limit_bytes=48 * 1024 * 1024)


def cut(shape, width):
    lead = (0,) * (len(shape) - 1)
    if shape == (1,):
        return pl.BlockSpec(memory_space=pltpu.SMEM)
    if shape[-1] != width:
        return pl.BlockSpec(shape, lambda i: lead + (0,))
    return pl.BlockSpec(shape[:-1] + (TILE,), lambda i: lead + (i,))


def call(kernel, width, ins, outs, scratch, weight=1):
    return pl.pallas_call(
        kernel,
        grid=(width // TILE,),
        in_specs=[cut(a.shape, width) for a in ins],
        out_specs=[cut(shape, width) for shape, _ in outs],
        out_shape=[jax.ShapeDtypeStruct(shape, kind) for shape, kind in outs],
        scratch_shapes=scratch,
        compiler_params=PARAMS,
        cost_estimate=pl.CostEstimate(
            flops=weight * 192 * KERNEL * width * 4, bytes_accessed=4 * 224 * width * 4, transcendentals=0
        ),
    )(*ins)


def local(frame_counts, glu_out, tap_weight, bn_gain, bn_shift, proj_weight, out_grad):
    inputs = glu_out[0]
    grads_in = out_grad[0]
    frames, width = inputs.shape
    half_width = width // 2
    devices = lax.axis_size(SEQ)
    chips, column = lax.axis_size(PLANE), lax.axis_size(COLUMN)
    total_rows = frames * chips * column
    core = lax.axis_index("c")
    rows = frames + 2 * HALF
    reach = frames + 4 * HALF - SUB
    bf16 = jnp.bfloat16

    up = jnp.concatenate([inputs[-2 * HALF :], grads_in[-HALF:]])
    down = jnp.concatenate([inputs[: 2 * HALF], grads_in[:HALF]])
    low, high = shifted(up, SEQ, 1), shifted(down, SEQ, -1)
    grads_wide = jnp.concatenate([low[2 * HALF :], grads_in, high[2 * HALF :]])

    first = lax.axis_index(SEQ) * frames - 2 * HALF
    positions = first + jnp.arange(frames + 4 * HALF, dtype=jnp.int32)
    segments = segment_ids(frame_counts[0], positions, frames * devices)
    segments = jnp.broadcast_to(segments[:, None], (frames + 4 * HALF, LANES))
    affine = jnp.stack([bn_gain, bn_shift])
    value_copies = pltpu.VMEM((SUB, reach, TILE), F32)
    id_copies = pltpu.VMEM((SUB, reach, LANES), jnp.int32)
    column_rows = pltpu.VMEM((frames, TILE), F32)

    conv, own_stats, sent = call(
        conv_kernel, width, [low, inputs, high, segments, tap_weight],
        [((rows, width), F32), ((2, width), F32), ((chips, 2, width), F32)],
        [value_copies, id_copies],
    )
    back = lax.dot_general(
        grads_wide, proj_weight, (((1,), (1,)), ((), ())), preferred_element_type=F32
    )
    sent, back, grads_in = lax.optimization_barrier((exchanged(sent, PLANE), back, grads_in))
    mine = lax.dynamic_slice_in_dim(grads_in, core * half_width, half_width, 1)
    other = lax.dynamic_slice_in_dim(grads_in, (1 - core) * half_width, half_width, 1)
    other = rotated(other, "c", 1)
    stats, conv = lax.optimization_barrier((merged(sent, frames), conv))
    (product,) = call(
        moments_kernel, width, [low, inputs, high, segments, conv, own_stats], [((KERNEL, width), F32)],
        [value_copies, id_copies, column_rows],
    )
    wide = jnp.concatenate([low[: 2 * HALF], inputs, high[: 2 * HALF]])
    plain = jnp.dot(
        window_mask(frame_counts[0], first, frames, frames * devices), wide, preferred_element_type=F32
    )
    stats = gathered(stats, COLUMN)

    swished, act_grad, kept, given, norm = call(
        functools.partial(act_kernel, frames * chips), width,
        [core.reshape(1), low, inputs, high, segments, conv, back, stats, own_stats, affine, plain, product],
        [((frames, width), bf16), ((rows, width), F32), ((chips, 4, width), F32), ((chips, 4, width), F32),
         ((2, width), F32)],
        [value_copies, id_copies, column_rows, pltpu.VMEM((KERNEL, TILE), F32)],
    )
    sent, swished = lax.optimization_barrier((kept + rotated(given, "c", 1), swished))
    sent = exchanged(sent, PLANE)

    share = width // chips
    quarter = half_width // 2
    height = share + 16
    left, right = pl.pallas_call(
        weight_kernel,
        grid=(4,),
        in_specs=[pl.BlockSpec((frames, width // 4), lambda i: (0, i))] * 2
        + [pl.BlockSpec((frames, half_width), lambda i: (0, 0))] * 2,
        out_specs=[pl.BlockSpec((chips // 4, n, quarter), lambda i: (i, 0, 0)) for n in (share, height)],
        out_shape=[jax.ShapeDtypeStruct((chips, n, quarter), bf16) for n in (share, height)],
        compiler_params=PARAMS,
        cost_estimate=pl.CostEstimate(
            flops=4 * frames * width * half_width, bytes_accessed=6 * width * half_width, transcendentals=0
        ),
    )(swished, rotated(swished, "c", 1), mine, other)
    block = jnp.dot(swished, proj_weight, preferred_element_type=F32).astype(bf16)
    sent, left, right = lax.optimization_barrier((sent, left, right))
    left = exchanged(left, PLANE)

    sent = jnp.sum(sent, axis=0)
    bit = 1
    while bit < lax.axis_size("z"):
        sent = sent + crossed(sent, "z", bit)
        bit *= 2
    sums = doubled(sent[3:], "c", 1)
    sums, sent, left, right = lax.optimization_barrier((sums, sent, left, right))
    right = pl.pallas_call(
        functools.partial(tap_kernel, total_rows),
        grid=(1,),
        in_specs=[cut(a.shape, 0) for a in (sent, sums, norm, affine)] + [pl.BlockSpec(memory_space=pl.ANY)],
        out_specs=pl.BlockSpec((chips, height - share, quarter), lambda i: (0, share // (height - share), 0)),
        out_shape=jax.ShapeDtypeStruct(right.shape, bf16),
        input_output_aliases={4: 0},
        compiler_params=PARAMS,
    )(sent, sums, norm, affine, right)
    right = exchanged(right, PLANE)

    (frame_grad,) = call(
        functools.partial(frame_kernel, total_rows), width,
        [segments, conv, act_grad, norm, sums, affine, tap_weight], [((frames, width), bf16)],
        [value_copies, id_copies, column_rows],
    )
    right, frame_grad, block = lax.optimization_barrier((right, frame_grad, block))
    part, tap_grad = pl.pallas_call(
        collect_kernel,
        grid=(1,),
        in_specs=[cut(left.shape, 0), cut(right.shape, 0)],
        out_specs=[cut((column, share // column, half_width), 0), cut((chips, width), 0)],
        out_shape=[
            jax.ShapeDtypeStruct((column, share // column, half_width), F32),
            jax.ShapeDtypeStruct((chips, width), F32),
        ],
        compiler_params=PARAMS,
    )(left, right)
    tap_grad = doubled(tap_grad, "c", 1)
    part = exchanged(part, COLUMN)
    part = jnp.sum(part.reshape((2, column // 2) + part.shape[1:]), axis=1)
    proj_grad = jnp.concatenate([part[0], part[1]], axis=1)
    return (block[None], frame_grad[None], tap_grad, sums[1], sums[0], proj_grad)


def solution(mesh):
    grid = Mesh(mesh.devices.reshape(4, 4, 2, -1), ("x", "y", "c", "z"))
    wide = P("z", SEQ, None)
    return jax.shard_map(
        local,
        mesh=grid,
        in_specs=(P("z", None), wide, P(), P(), P(), P(), wide),
        out_specs=(wide, wide, P(), P(), P(), P(("x", "y", "c", "z"), None)),
        check_vma=False,
    )
```

```python
import functools

import jax
import jax.numpy as jnp
from jax import lax
from jax.experimental import pallas as pl
from jax.experimental.pallas import tpu as pltpu
from jax.sharding import Mesh, PartitionSpec as P

HALF = 16
KERNEL = 2 * HALF
EPSILON = 1e-05
SEQ = ("x", "y", "c")
PLANE = ("x", "y")
COLUMN = ("c", "z")
LANES = 128
TILE = 512
SUB = 8
BLOCKS = 4
GROUP = 4
F32 = jnp.float32


def shifted(value, axes, step):
    count = lax.axis_size(axes)
    pairs = [(i, i + step) for i in range(count) if 0 <= i + step < count]
    return lax.ppermute(value, axes, pairs)


def rotated(value, axis, step):
    count = lax.axis_size(axis)
    return lax.ppermute(value, axis, [(i, (i + step) % count) for i in range(count)])


def crossed(value, axis, bit):
    count = lax.axis_size(axis)
    return lax.ppermute(value, axis, [(i, i ^ bit) for i in range(count)])


def doubled(value, axis, bit):
    other = crossed(value, axis, bit)
    upper = (lax.axis_index(axis) & bit) != 0
    first, second = jnp.where(upper, other, value), jnp.where(upper, value, other)
    return jnp.concatenate([first, second])


def exchanged(blocks, axes):
    return lax.all_to_all(blocks, axes, 0, 0, tiled=True)


def gathered(value, axes):
    count = lax.axis_size(axes)
    return exchanged(jnp.broadcast_to(value[None], (count,) + value.shape), axes)


def merged(stats, count):
    means, squares = stats[:, 0], stats[:, 1]
    mean = jnp.mean(means, axis=0)
    spread = jnp.sum(jnp.square(means - mean), axis=0)
    return jnp.stack([mean, jnp.sum(squares, axis=0) + count * spread])


def segment_ids(counts, positions, frames):
    ends = jnp.cumsum(counts)
    found = jnp.sum((positions[:, None] >= ends[None, :]).astype(jnp.int32), axis=1)
    return jnp.where((positions >= 0) & (positions < frames), found, -1)


def window_mask(counts, first, frames, limit):
    row = lax.broadcasted_iota(jnp.int32, (KERNEL, frames + 4 * HALF), 1)
    owner = row + HALF - lax.broadcasted_iota(jnp.int32, row.shape, 0)
    ends = jnp.cumsum(counts)[:, None, None]
    same = jnp.all((first + row >= ends) == (first + owner >= ends), axis=0)
    inside = (owner >= 2 * HALF) & (owner < 2 * HALF + frames)
    valid = (first + row >= 0) & (first + row < limit)
    return (same & inside & valid).astype(jnp.bfloat16)


def shift_copies(source, copies):
    rows = copies.shape[1]
    for b in range(SUB):
        copies[b] = source[b : b + rows]


def lane_groups():
    tiles = [pl.ds(t * LANES, LANES) for t in range(TILE // LANES)]
    return [tiles[t : t + GROUP] for t in range(0, len(tiles), GROUP)]


def convolve(ids_ref, ids, copies, taps_ref, out_ref, rows, centre, tap_of, id_shift):
    offsets = [o for o in range(KERNEL + 1) if 0 <= tap_of(o) < KERNEL]
    for tiles in lane_groups():
        def step(j, carry, tiles=tiles):
            base = pl.multiple_of(j * SUB * BLOCKS, SUB * BLOCKS)
            own = [ids_ref[pl.ds(base + i * SUB + centre, SUB), :] for i in range(BLOCKS)]
            totals = [[jnp.zeros((SUB, LANES), F32) for _ in tiles] for _ in range(BLOCKS)]
            for low in range(SUB):
                steps = [o // SUB for o in offsets if o % SUB == low]
                reads = range(min(steps), max(steps) + BLOCKS)
                near = {i: ids[low, pl.ds(base + i * SUB + id_shift, SUB), :] for i in reads}
                keep = {(a, i): near[a + i] == own[i] for a in steps for i in range(BLOCKS)}
                for t, lanes in enumerate(tiles):
                    value = {i: copies[low, pl.ds(base + i * SUB, SUB), lanes] for i in reads}
                    for a in steps:
                        tap = taps_ref[pl.ds(tap_of(a * SUB + low), 1), lanes]
                        for i in range(BLOCKS):
                            term = jnp.where(keep[a, i], value[a + i], 0.0)
                            totals[i][t] = totals[i][t] + tap * term
            for i in range(BLOCKS):
                for t, lanes in enumerate(tiles):
                    out_ref[pl.ds(base + i * SUB, SUB), lanes] = totals[i][t]
            return carry

        lax.fori_loop(0, rows // (SUB * BLOCKS), step, 0)


def correlate(grad_ref, ids_ref, ids, copies, rows, first, out_ref):
    steps = range(KERNEL // SUB)
    for tiles in lane_groups():
        for low in range(SUB):
            def step(j, sums, tiles=tiles, low=low):
                base = pl.multiple_of(j * SUB * BLOCKS, SUB * BLOCKS)
                reads = range(len(steps) + BLOCKS - 1)
                own = [ids_ref[pl.ds(base + i * SUB + first + HALF, SUB), :] for i in range(BLOCKS)]
                near = [ids[low, pl.ds(base + i * SUB + first, SUB), :] for i in reads]
                keep = {(a, i): near[a + i] == own[i] for a in steps for i in range(BLOCKS)}
                out = list(sums)
                for t, lanes in enumerate(tiles):
                    value = [copies[low, pl.ds(base + i * SUB + first, SUB), lanes] for i in reads]
                    grads = [grad_ref[pl.ds(base + i * SUB, SUB), lanes] for i in range(BLOCKS)]
                    for a in steps:
                        at = t * len(steps) + a
                        for i in range(BLOCKS):
                            out[at] = out[at] + jnp.where(keep[a, i], value[a + i], 0.0) * grads[i]
                return tuple(out)

            start = tuple(jnp.zeros((SUB, LANES), F32) for _ in range(len(steps) * len(tiles)))
            sums = lax.fori_loop(0, rows // (SUB * BLOCKS), step, start)
            for t, lanes in enumerate(tiles):
                for a in steps:
                    total = jnp.sum(sums[t * len(steps) + a], axis=0, keepdims=True)
                    out_ref[pl.ds(a * SUB + low, 1), lanes] = total


def prepare(low_ref, mid_ref, high_ref, ids_ref, copies, ids):
    @pl.when(pl.program_id(0) == 0)
    def _():
        shift_copies(ids_ref[...], ids)

    parts = [low_ref[...][: 2 * HALF], mid_ref[...], high_ref[...][: 2 * HALF]]
    shift_copies(jnp.concatenate([p.astype(F32) for p in parts]), copies)


def conv_kernel(low_ref, mid_ref, high_ref, ids_ref, taps_ref, conv_ref, stats_ref, sent_ref, copies, ids):
    rows = conv_ref.shape[0]
    prepare(low_ref, mid_ref, high_ref, ids_ref, copies, ids)
    convolve(ids_ref, ids, copies, taps_ref, conv_ref, rows, HALF, lambda o: o, 0)
    inner = conv_ref[HALF : rows - HALF, :]
    mean = jnp.sum(inner, axis=0, keepdims=True) / inner.shape[0]
    stats = jnp.concatenate([mean, jnp.sum(jnp.square(inner - mean), axis=0, keepdims=True)])
    stats_ref[...] = stats
    sent_ref[...] = jnp.broadcast_to(stats[None], sent_ref.shape)


def moments_kernel(
    low_ref, mid_ref, high_ref, ids_ref, conv_ref, stats_ref, out_ref, copies, ids, centred
):
    rows = conv_ref.shape[0] - 2 * HALF
    prepare(low_ref, mid_ref, high_ref, ids_ref, copies, ids)
    centred[...] = conv_ref[HALF : HALF + rows, :] - stats_ref[0:1, :]
    correlate(centred, ids_ref, ids, copies, rows, HALF, out_ref)


def act_kernel(
    count, core_ref, low_ref, mid_ref, high_ref, ids_ref, conv_ref, back_ref, all_ref, own_ref, affine_ref,
    plain_ref, product_ref, swished_ref, grad_ref, kept_ref, given_ref, norm_ref, copies, ids, centred, taps,
):
    rows = conv_ref.shape[0] - 2 * HALF
    prepare(low_ref, mid_ref, high_ref, ids_ref, copies, ids)
    merge = all_ref.shape[0]
    means = [all_ref[i, 0:1, :] for i in range(merge)]
    mean = sum(means) / merge
    spread = sum(jnp.square(m - mean) for m in means)
    var = (sum(all_ref[i, 1:2, :] for i in range(merge)) + count * spread) / (count * merge)
    inverse = lax.rsqrt(var + EPSILON)
    norm_ref[...] = jnp.concatenate([mean, inverse])
    normed = (conv_ref[...] - mean) * inverse
    act = affine_ref[0:1, :] * normed + affine_ref[1:2, :]
    gate = jax.nn.sigmoid(act)
    grad = back_ref[...] * gate * (1.0 + act * (1.0 - gate))
    grad_ref[...] = grad
    swished_ref[...] = (act * gate)[HALF : HALF + rows].astype(jnp.bfloat16)
    inner, inner_normed = grad[HALF : HALF + rows], normed[HALF : HALF + rows]
    sums = [jnp.sum(inner, axis=0, keepdims=True), jnp.sum(inner * inner_normed, axis=0, keepdims=True)]
    centred[...] = inner
    correlate(centred, ids_ref, ids, copies, rows, HALF, taps)
    plain = plain_ref[...]
    product = inverse * (product_ref[...] + (own_ref[0:1, :] - mean) * plain)
    chips = kept_ref.shape[0]
    first = core_ref[0] == 0
    for i in range(chips):
        low, high = (
            jnp.concatenate([v[at : at + 1] for v in (taps, plain, product)] + [sums[at // chips]])
            for at in (i, chips + i)
        )
        kept_ref[i] = jnp.where(first, low, high)
        given_ref[i] = jnp.where(first, high, low)


def weight_kernel(_, own_ref, other_ref, own_grad_ref, other_grad_ref, left_ref, right_ref):
    over = (((0,), (0,)), ((), ()))
    part = lax.dot_general(own_ref[...], own_grad_ref[...], over, preferred_element_type=F32)
    part = part + lax.dot_general(other_ref[...], other_grad_ref[...], over, preferred_element_type=F32)
    part = part.astype(jnp.bfloat16)
    each, left = left_ref.shape[1:]
    for i in range(left_ref.shape[0]):
        left_ref[i] = part[i * each : (i + 1) * each, :left]
        right_ref[i, 0:each, :] = part[i * each : (i + 1) * each, left:]


def tap_kernel(total_rows, parts_ref, sums_ref, norm_ref, affine_ref, _, out_ref):
    scale = affine_ref[0:1, :] * norm_ref[1:2, :]
    shift, slope = sums_ref[0:1, :] / total_rows, sums_ref[1:2, :] / total_rows
    rest = scale * (parts_ref[0:1, :] - shift * parts_ref[1:2, :] - slope * parts_ref[2:3, :])
    height, size = out_ref.shape[1:]
    rows = []
    for _ in range(2):
        term = rest.astype(jnp.bfloat16).astype(F32)
        rows += [term[:, at : at + size] for at in range(0, rest.shape[1], size)]
        rest = rest - term
    rows.append(jnp.zeros((height - len(rows), size), F32))
    rows = jnp.concatenate(rows).astype(jnp.bfloat16)
    for i in range(out_ref.shape[0]):
        out_ref[i] = rows


def collect_kernel(left_ref, right_ref, out_ref, taps_ref):
    each = out_ref.shape[1]
    rows, left = left_ref.shape[1:]
    size = right_ref.shape[2]
    for all_ref, columns in ((left_ref, slice(0, left)), (right_ref, slice(left, left + size))):
        total = sum(all_ref[i, 0:rows, :].astype(F32) for i in range(all_ref.shape[0]))
        for i in range(out_ref.shape[0]):
            out_ref[i, :, columns] = total[i * each : (i + 1) * each]
    pieces = taps_ref.shape[1] // size
    for i in range(right_ref.shape[0]):
        terms = right_ref[i, rows:, :].astype(F32)
        terms = terms[:pieces] + terms[pieces : 2 * pieces]
        for piece in range(pieces):
            taps_ref[i : i + 1, piece * size : (piece + 1) * size] = terms[piece : piece + 1]


def frame_kernel(
    total_rows, ids_ref, conv_ref, grad_ref, norm_ref, sums_ref, affine_ref, taps_ref, out_ref, copies, ids, result
):
    rows = out_ref.shape[0]

    @pl.when(pl.program_id(0) == 0)
    def _():
        shift_copies(ids_ref[...], ids)

    mean, inverse = norm_ref[0:1, :], norm_ref[1:2, :]
    scale = affine_ref[0:1, :] * inverse
    shift, slope = sums_ref[0:1, :] / total_rows, sums_ref[1:2, :] / total_rows
    normed = (conv_ref[...] - mean) * inverse
    grad = scale * (grad_ref[...] - shift - normed * slope)
    for b in range(SUB):
        count = rows + 2 * HALF - (SUB if b else 0)
        copies[b, 0:count, :] = grad[b : b + count]

    convolve(
        ids_ref, ids, copies, taps_ref, result, rows, 2 * HALF, lambda o: KERNEL - o, HALF
    )
    out_ref[...] = result[...].astype(jnp.bfloat16)


PARAMS = pltpu.CompilerParams(vmem_limit_bytes=48 * 1024 * 1024)


def cut(shape, width):
    lead = (0,) * (len(shape) - 1)
    if shape == (1,):
        return pl.BlockSpec(memory_space=pltpu.SMEM)
    if shape[-1] != width:
        return pl.BlockSpec(shape, lambda i: lead + (0,))
    return pl.BlockSpec(shape[:-1] + (TILE,), lambda i: lead + (i,))


def call(kernel, width, ins, outs, scratch, weight=1):
    return pl.pallas_call(
        kernel,
        grid=(width // TILE,),
        in_specs=[cut(a.shape, width) for a in ins],
        out_specs=[cut(shape, width) for shape, _ in outs],
        out_shape=[jax.ShapeDtypeStruct(shape, kind) for shape, kind in outs],
        scratch_shapes=scratch,
        compiler_params=PARAMS,
        cost_estimate=pl.CostEstimate(
            flops=weight * 192 * KERNEL * width * 4, bytes_accessed=4 * 224 * width * 4, transcendentals=0
        ),
    )(*ins)


def local(frame_counts, glu_out, tap_weight, bn_gain, bn_shift, proj_weight, out_grad):
    inputs = glu_out[0]
    grads_in = out_grad[0]
    frames, width = inputs.shape
    half_width = width // 2
    devices = lax.axis_size(SEQ)
    chips, column = lax.axis_size(PLANE), lax.axis_size(COLUMN)
    total_rows = frames * chips * column
    core = lax.axis_index("c")
    rows = frames + 2 * HALF
    reach = frames + 4 * HALF - SUB
    bf16 = jnp.bfloat16

    up = jnp.concatenate([inputs[-2 * HALF :], grads_in[-HALF:]])
    down = jnp.concatenate([inputs[: 2 * HALF], grads_in[:HALF]])
    low, high = shifted(up, SEQ, 1), shifted(down, SEQ, -1)
    grads_wide = jnp.concatenate([low[2 * HALF :], grads_in, high[2 * HALF :]])

    first = lax.axis_index(SEQ) * frames - 2 * HALF
    positions = first + jnp.arange(frames + 4 * HALF, dtype=jnp.int32)
    segments = segment_ids(frame_counts[0], positions, frames * devices)
    segments = jnp.broadcast_to(segments[:, None], (frames + 4 * HALF, LANES))
    affine = jnp.stack([bn_gain, bn_shift])
    value_copies = pltpu.VMEM((SUB, reach, TILE), F32)
    id_copies = pltpu.VMEM((SUB, reach, LANES), jnp.int32)
    column_rows = pltpu.VMEM((frames, TILE), F32)

    conv, own_stats, sent = call(
        conv_kernel, width, [low, inputs, high, segments, tap_weight],
        [((rows, width), F32), ((2, width), F32), ((chips, 2, width), F32)],
        [value_copies, id_copies],
    )
    (product,) = call(
        moments_kernel, width, [low, inputs, high, segments, conv, own_stats], [((KERNEL, width), F32)],
        [value_copies, id_copies, column_rows],
    )
    sent, product = lax.optimization_barrier((exchanged(sent, PLANE), product))
    stats, grads_wide, grads_in = lax.optimization_barrier((merged(sent, frames), grads_wide, grads_in))
    back = lax.dot_general(
        grads_wide, proj_weight, (((1,), (1,)), ((), ())), preferred_element_type=F32
    )
    wide = jnp.concatenate([low[: 2 * HALF], inputs, high[: 2 * HALF]])
    plain = jnp.dot(
        window_mask(frame_counts[0], first, frames, frames * devices), wide, preferred_element_type=F32
    )
    stats = gathered(stats, COLUMN)

    swished, act_grad, kept, given, norm = call(
        functools.partial(act_kernel, frames * chips), width,
        [core.reshape(1), low, inputs, high, segments, conv, back, stats, own_stats, affine, plain, product],
        [((frames, width), bf16), ((rows, width), F32), ((chips, 4, width), F32), ((chips, 4, width), F32),
         ((2, width), F32)],
        [value_copies, id_copies, column_rows, pltpu.VMEM((KERNEL, TILE), F32)],
    )
    sent, swished = lax.optimization_barrier((kept + rotated(given, "c", 1), swished))
    sent = exchanged(sent, PLANE)

    share = width // chips
    right_width = half_width // 3
    left_width = half_width - right_width
    height = share + 16
    left, right = pl.pallas_call(
        weight_kernel,
        grid_spec=pltpu.PrefetchScalarGridSpec(
            num_scalar_prefetch=1,
            grid=(4,),
            in_specs=[pl.BlockSpec((frames, width // 4), lambda i, own: (0, i))] * 2
            + [pl.BlockSpec((frames, half_width), lambda i, own: (0, own[0]))] * 2,
            out_specs=[
                pl.BlockSpec((chips // 4, share, left_width), lambda i, own: (i, 0, 0)),
                pl.BlockSpec((chips // 4, height, right_width), lambda i, own: (i, 0, 0)),
            ],
        ),
        out_shape=[
            jax.ShapeDtypeStruct((chips, share, left_width), bf16),
            jax.ShapeDtypeStruct((chips, height, right_width), bf16),
        ],
        compiler_params=PARAMS,
        cost_estimate=pl.CostEstimate(
            flops=4 * frames * width * half_width, bytes_accessed=6 * width * half_width, transcendentals=0
        ),
    )(core.reshape(1), swished, rotated(swished, "c", 1), grads_in, rotated(grads_in, "c", 1))
    block = jnp.dot(swished, proj_weight, preferred_element_type=F32).astype(bf16)
    sent, left, right = lax.optimization_barrier((sent, left, right))
    left = exchanged(left, PLANE)

    sent = jnp.sum(sent, axis=0)
    bit = 1
    while bit < lax.axis_size("z"):
        sent = sent + crossed(sent, "z", bit)
        bit *= 2
    sums = doubled(sent[3:], "c", 1)
    sums, sent, left, right = lax.optimization_barrier((sums, sent, left, right))
    right = pl.pallas_call(
        functools.partial(tap_kernel, total_rows),
        grid=(1,),
        in_specs=[cut(a.shape, 0) for a in (sent, sums, norm, affine)] + [pl.BlockSpec(memory_space=pl.ANY)],
        out_specs=pl.BlockSpec((chips, height - share, right_width), lambda i: (0, share // (height - share), 0)),
        out_shape=jax.ShapeDtypeStruct(right.shape, bf16),
        input_output_aliases={4: 0},
        compiler_params=PARAMS,
    )(sent, sums, norm, affine, right)
    right = exchanged(right, PLANE)

    (frame_grad,) = call(
        functools.partial(frame_kernel, total_rows), width,
        [segments, conv, act_grad, norm, sums, affine, tap_weight], [((frames, width), bf16)],
        [value_copies, id_copies, column_rows],
    )
    right, frame_grad, block = lax.optimization_barrier((right, frame_grad, block))
    part, tap_grad = pl.pallas_call(
        collect_kernel,
        grid=(1,),
        in_specs=[cut(left.shape, 0), cut(right.shape, 0)],
        out_specs=[cut((column, share // column, half_width), 0), cut((chips, width), 0)],
        out_shape=[
            jax.ShapeDtypeStruct((column, share // column, half_width), F32),
            jax.ShapeDtypeStruct((chips, width), F32),
        ],
        compiler_params=PARAMS,
    )(left, right)
    tap_grad = doubled(tap_grad, "c", 1)
    part = exchanged(part, COLUMN)
    part = jnp.sum(part.reshape((2, column // 2) + part.shape[1:]), axis=1)
    proj_grad = jnp.concatenate([part[0], part[1]], axis=1)
    return (block[None], frame_grad[None], tap_grad, sums[1], sums[0], proj_grad)


def solution(mesh):
    grid = Mesh(mesh.devices.reshape(4, 4, 2, -1), ("x", "y", "c", "z"))
    wide = P("z", SEQ, None)
    return jax.shard_map(
        local,
        mesh=grid,
        in_specs=(P("z", None), wide, P(), P(), P(), P(), wide),
        out_specs=(wide, wide, P(), P(), P(), P(("x", "y", "c", "z"), None)),
        check_vma=False,
    )
```

```python
import functools

import jax
import jax.numpy as jnp
from jax import lax
from jax.experimental import pallas as pl
from jax.experimental.pallas import tpu as pltpu
from jax.sharding import Mesh, PartitionSpec as P

HALF = 16
KERNEL = 2 * HALF
EPSILON = 1e-05
SEQ = ("x", "y", "c")
PLANE = ("x", "y")
COLUMN = ("c", "z")
LANES = 128
TILE = 512
SUB = 8
BLOCKS = 4
GROUP = 4
F32 = jnp.float32


def shifted(value, axes, step):
    count = lax.axis_size(axes)
    pairs = [(i, i + step) for i in range(count) if 0 <= i + step < count]
    return lax.ppermute(value, axes, pairs)


def rotated(value, axis, step):
    count = lax.axis_size(axis)
    return lax.ppermute(value, axis, [(i, (i + step) % count) for i in range(count)])


def crossed(value, axis, bit):
    count = lax.axis_size(axis)
    return lax.ppermute(value, axis, [(i, i ^ bit) for i in range(count)])


def doubled(value, axis, bit):
    other = crossed(value, axis, bit)
    upper = (lax.axis_index(axis) & bit) != 0
    first, second = jnp.where(upper, other, value), jnp.where(upper, value, other)
    return jnp.concatenate([first, second])


def exchanged(blocks, axes):
    return lax.all_to_all(blocks, axes, 0, 0, tiled=True)


def gathered(value, axes):
    count = lax.axis_size(axes)
    return exchanged(jnp.broadcast_to(value[None], (count,) + value.shape), axes)


def merged(stats, count):
    means, squares = stats[:, 0], stats[:, 1]
    mean = jnp.mean(means, axis=0)
    spread = jnp.sum(jnp.square(means - mean), axis=0)
    return jnp.stack([mean, jnp.sum(squares, axis=0) + count * spread])


def segment_ids(counts, positions, frames):
    ends = jnp.cumsum(counts)
    found = jnp.sum((positions[:, None] >= ends[None, :]).astype(jnp.int32), axis=1)
    return jnp.where((positions >= 0) & (positions < frames), found, -1)


def window_mask(counts, first, frames, limit):
    row = lax.broadcasted_iota(jnp.int32, (KERNEL, frames + 4 * HALF), 1)
    owner = row + HALF - lax.broadcasted_iota(jnp.int32, row.shape, 0)
    ends = jnp.cumsum(counts)[:, None, None]
    same = jnp.all((first + row >= ends) == (first + owner >= ends), axis=0)
    inside = (owner >= 2 * HALF) & (owner < 2 * HALF + frames)
    valid = (first + row >= 0) & (first + row < limit)
    return (same & inside & valid).astype(jnp.bfloat16)


def shift_copies(source, copies):
    rows = copies.shape[1]
    for b in range(SUB):
        copies[b] = source[b : b + rows]


def lane_groups():
    tiles = [pl.ds(t * LANES, LANES) for t in range(TILE // LANES)]
    return [tiles[t : t + GROUP] for t in range(0, len(tiles), GROUP)]


def convolve(ids_ref, ids, copies, taps_ref, out_ref, rows, centre, tap_of, id_shift):
    offsets = [o for o in range(KERNEL + 1) if 0 <= tap_of(o) < KERNEL]
    for tiles in lane_groups():
        def step(j, carry, tiles=tiles):
            base = pl.multiple_of(j * SUB * BLOCKS, SUB * BLOCKS)
            own = [ids_ref[pl.ds(base + i * SUB + centre, SUB), :] for i in range(BLOCKS)]
            totals = [[jnp.zeros((SUB, LANES), F32) for _ in tiles] for _ in range(BLOCKS)]
            for low in range(SUB):
                steps = [o // SUB for o in offsets if o % SUB == low]
                reads = range(min(steps), max(steps) + BLOCKS)
                near = {i: ids[low, pl.ds(base + i * SUB + id_shift, SUB), :] for i in reads}
                keep = {(a, i): near[a + i] == own[i] for a in steps for i in range(BLOCKS)}
                for t, lanes in enumerate(tiles):
                    value = {i: copies[low, pl.ds(base + i * SUB, SUB), lanes] for i in reads}
                    for a in steps:
                        tap = taps_ref[pl.ds(tap_of(a * SUB + low), 1), lanes]
                        for i in range(BLOCKS):
                            term = jnp.where(keep[a, i], value[a + i], 0.0)
                            totals[i][t] = totals[i][t] + tap * term
            for i in range(BLOCKS):
                for t, lanes in enumerate(tiles):
                    out_ref[pl.ds(base + i * SUB, SUB), lanes] = totals[i][t]
            return carry

        lax.fori_loop(0, rows // (SUB * BLOCKS), step, 0)


def correlate(grad_ref, ids_ref, ids, copies, rows, first, out_ref):
    steps = range(KERNEL // SUB)
    for tiles in lane_groups():
        for low in range(SUB):
            def step(j, sums, tiles=tiles, low=low):
                base = pl.multiple_of(j * SUB * BLOCKS, SUB * BLOCKS)
                reads = range(len(steps) + BLOCKS - 1)
                own = [ids_ref[pl.ds(base + i * SUB + first + HALF, SUB), :] for i in range(BLOCKS)]
                near = [ids[low, pl.ds(base + i * SUB + first, SUB), :] for i in reads]
                keep = {(a, i): near[a + i] == own[i] for a in steps for i in range(BLOCKS)}
                out = list(sums)
                for t, lanes in enumerate(tiles):
                    value = [copies[low, pl.ds(base + i * SUB + first, SUB), lanes] for i in reads]
                    grads = [grad_ref[pl.ds(base + i * SUB, SUB), lanes] for i in range(BLOCKS)]
                    for a in steps:
                        at = t * len(steps) + a
                        for i in range(BLOCKS):
                            out[at] = out[at] + jnp.where(keep[a, i], value[a + i], 0.0) * grads[i]
                return tuple(out)

            start = tuple(jnp.zeros((SUB, LANES), F32) for _ in range(len(steps) * len(tiles)))
            sums = lax.fori_loop(0, rows // (SUB * BLOCKS), step, start)
            for t, lanes in enumerate(tiles):
                for a in steps:
                    total = jnp.sum(sums[t * len(steps) + a], axis=0, keepdims=True)
                    out_ref[pl.ds(a * SUB + low, 1), lanes] = total


def prepare(low_ref, mid_ref, high_ref, ids_ref, copies, ids):
    @pl.when(pl.program_id(0) == 0)
    def _():
        shift_copies(ids_ref[...], ids)

    parts = [low_ref[...][: 2 * HALF], mid_ref[...], high_ref[...][: 2 * HALF]]
    shift_copies(jnp.concatenate([p.astype(F32) for p in parts]), copies)


def conv_kernel(low_ref, mid_ref, high_ref, ids_ref, taps_ref, conv_ref, stats_ref, sent_ref, copies, ids):
    rows = conv_ref.shape[0]
    prepare(low_ref, mid_ref, high_ref, ids_ref, copies, ids)
    convolve(ids_ref, ids, copies, taps_ref, conv_ref, rows, HALF, lambda o: o, 0)
    inner = conv_ref[HALF : rows - HALF, :]
    mean = jnp.sum(inner, axis=0, keepdims=True) / inner.shape[0]
    stats = jnp.concatenate([mean, jnp.sum(jnp.square(inner - mean), axis=0, keepdims=True)])
    stats_ref[...] = stats
    sent_ref[...] = jnp.broadcast_to(stats[None], sent_ref.shape)


def moments_kernel(
    low_ref, mid_ref, high_ref, ids_ref, conv_ref, stats_ref, out_ref, copies, ids, centred
):
    rows = conv_ref.shape[0] - 2 * HALF
    prepare(low_ref, mid_ref, high_ref, ids_ref, copies, ids)
    centred[...] = conv_ref[HALF : HALF + rows, :] - stats_ref[0:1, :]
    correlate(centred, ids_ref, ids, copies, rows, HALF, out_ref)


def act_kernel(
    count, core_ref, low_ref, mid_ref, high_ref, ids_ref, conv_ref, back_ref, all_ref, own_ref, affine_ref,
    plain_ref, product_ref, swished_ref, grad_ref, kept_ref, given_ref, norm_ref, copies, ids, centred, taps,
):
    rows = conv_ref.shape[0] - 2 * HALF
    prepare(low_ref, mid_ref, high_ref, ids_ref, copies, ids)
    merge = all_ref.shape[0]
    means = [all_ref[i, 0:1, :] for i in range(merge)]
    mean = sum(means) / merge
    spread = sum(jnp.square(m - mean) for m in means)
    var = (sum(all_ref[i, 1:2, :] for i in range(merge)) + count * spread) / (count * merge)
    inverse = lax.rsqrt(var + EPSILON)
    norm_ref[...] = jnp.concatenate([mean, inverse])
    normed = (conv_ref[...] - mean) * inverse
    act = affine_ref[0:1, :] * normed + affine_ref[1:2, :]
    gate = jax.nn.sigmoid(act)
    grad = back_ref[...] * gate * (1.0 + act * (1.0 - gate))
    grad_ref[...] = grad
    swished_ref[...] = (act * gate)[HALF : HALF + rows].astype(jnp.bfloat16)
    inner, inner_normed = grad[HALF : HALF + rows], normed[HALF : HALF + rows]
    sums = [jnp.sum(inner, axis=0, keepdims=True), jnp.sum(inner * inner_normed, axis=0, keepdims=True)]
    centred[...] = inner
    correlate(centred, ids_ref, ids, copies, rows, HALF, taps)
    plain = plain_ref[...]
    product = inverse * (product_ref[...] + (own_ref[0:1, :] - mean) * plain)
    chips = kept_ref.shape[0]
    first = core_ref[0] == 0
    for i in range(chips):
        low, high = (
            jnp.concatenate([v[at : at + 1] for v in (taps, plain, product)] + [sums[at // chips]])
            for at in (i, chips + i)
        )
        kept_ref[i] = jnp.where(first, low, high)
        given_ref[i] = jnp.where(first, high, low)


def weight_kernel(_, own_ref, other_ref, own_grad_ref, other_grad_ref, left_ref, right_ref):
    over = (((0,), (0,)), ((), ()))
    part = lax.dot_general(own_ref[...], own_grad_ref[...], over, preferred_element_type=F32)
    part = part + lax.dot_general(other_ref[...], other_grad_ref[...], over, preferred_element_type=F32)
    part = part.astype(jnp.bfloat16)
    each, left = left_ref.shape[1:]
    for i in range(left_ref.shape[0]):
        left_ref[i] = part[i * each : (i + 1) * each, :left]
        right_ref[i, 0:each, :] = part[i * each : (i + 1) * each, left:]


def tap_kernel(total_rows, parts_ref, sums_ref, norm_ref, affine_ref, _, out_ref):
    scale = affine_ref[0:1, :] * norm_ref[1:2, :]
    shift, slope = sums_ref[0:1, :] / total_rows, sums_ref[1:2, :] / total_rows
    rest = scale * (parts_ref[0:1, :] - shift * parts_ref[1:2, :] - slope * parts_ref[2:3, :])
    height, size = out_ref.shape[1:]
    rows = []
    for _ in range(2):
        term = rest.astype(jnp.bfloat16).astype(F32)
        rows += [term[:, at : at + size] for at in range(0, rest.shape[1], size)]
        rest = rest - term
    rows.append(jnp.zeros((height - len(rows), size), F32))
    rows = jnp.concatenate(rows).astype(jnp.bfloat16)
    for i in range(out_ref.shape[0]):
        out_ref[i] = rows


def collect_kernel(left_ref, right_ref, out_ref, taps_ref):
    each = out_ref.shape[1]
    rows, left = left_ref.shape[1:]
    size = right_ref.shape[2]
    for all_ref, columns in ((left_ref, slice(0, left)), (right_ref, slice(left, left + size))):
        total = sum(all_ref[i, 0:rows, :].astype(F32) for i in range(all_ref.shape[0]))
        for i in range(out_ref.shape[0]):
            out_ref[i, :, columns] = total[i * each : (i + 1) * each]
    pieces = taps_ref.shape[1] // size
    for i in range(right_ref.shape[0]):
        terms = right_ref[i, rows:, :].astype(F32)
        terms = terms[:pieces] + terms[pieces : 2 * pieces]
        for piece in range(pieces):
            taps_ref[i : i + 1, piece * size : (piece + 1) * size] = terms[piece : piece + 1]


def frame_kernel(
    total_rows, ids_ref, conv_ref, grad_ref, norm_ref, sums_ref, affine_ref, taps_ref, out_ref, copies, ids, result
):
    rows = out_ref.shape[0]

    @pl.when(pl.program_id(0) == 0)
    def _():
        shift_copies(ids_ref[...], ids)

    mean, inverse = norm_ref[0:1, :], norm_ref[1:2, :]
    scale = affine_ref[0:1, :] * inverse
    shift, slope = sums_ref[0:1, :] / total_rows, sums_ref[1:2, :] / total_rows
    normed = (conv_ref[...] - mean) * inverse
    grad = scale * (grad_ref[...] - shift - normed * slope)
    for b in range(SUB):
        count = rows + 2 * HALF - (SUB if b else 0)
        copies[b, 0:count, :] = grad[b : b + count]

    convolve(
        ids_ref, ids, copies, taps_ref, result, rows, 2 * HALF, lambda o: KERNEL - o, HALF
    )
    out_ref[...] = result[...].astype(jnp.bfloat16)


PARAMS = pltpu.CompilerParams(vmem_limit_bytes=16 * 1024 * 1024)


def cut(shape, width):
    lead = (0,) * (len(shape) - 1)
    if shape == (1,):
        return pl.BlockSpec(memory_space=pltpu.SMEM)
    if shape[-1] != width:
        return pl.BlockSpec(shape, lambda i: lead + (0,))
    return pl.BlockSpec(shape[:-1] + (TILE,), lambda i: lead + (i,))


def call(kernel, width, ins, outs, scratch, weight=1):
    return pl.pallas_call(
        kernel,
        grid=(width // TILE,),
        in_specs=[cut(a.shape, width) for a in ins],
        out_specs=[cut(shape, width) for shape, _ in outs],
        out_shape=[jax.ShapeDtypeStruct(shape, kind) for shape, kind in outs],
        scratch_shapes=scratch,
        compiler_params=PARAMS,
        cost_estimate=pl.CostEstimate(
            flops=weight * 192 * KERNEL * width * 4, bytes_accessed=4 * 224 * width * 4, transcendentals=0
        ),
    )(*ins)


def local(frame_counts, glu_out, tap_weight, bn_gain, bn_shift, proj_weight, out_grad):
    inputs = glu_out[0]
    grads_in = out_grad[0]
    frames, width = inputs.shape
    half_width = width // 2
    devices = lax.axis_size(SEQ)
    chips, column = lax.axis_size(PLANE), lax.axis_size(COLUMN)
    total_rows = frames * chips * column
    core = lax.axis_index("c")
    rows = frames + 2 * HALF
    reach = frames + 4 * HALF - SUB
    bf16 = jnp.bfloat16

    up = jnp.concatenate([inputs[-2 * HALF :], grads_in[-HALF:]])
    down = jnp.concatenate([inputs[: 2 * HALF], grads_in[:HALF]])
    low, high = shifted(up, SEQ, 1), shifted(down, SEQ, -1)
    grads_wide = jnp.concatenate([low[2 * HALF :], grads_in, high[2 * HALF :]])

    first = lax.axis_index(SEQ) * frames - 2 * HALF
    positions = first + jnp.arange(frames + 4 * HALF, dtype=jnp.int32)
    segments = segment_ids(frame_counts[0], positions, frames * devices)
    segments = jnp.broadcast_to(segments[:, None], (frames + 4 * HALF, LANES))
    value_copies = pltpu.VMEM((SUB, reach, TILE), F32)
    id_copies = pltpu.VMEM((SUB, reach, LANES), jnp.int32)
    column_rows = pltpu.VMEM((frames, TILE), F32)

    conv, own_stats, sent = call(
        conv_kernel, width, [low, inputs, high, segments, tap_weight],
        [((rows, width), F32), ((2, width), F32), ((chips, 2, width), F32)],
        [value_copies, id_copies],
    )
    back = lax.dot_general(
        grads_wide, proj_weight, (((1,), (1,)), ((), ())), preferred_element_type=F32
    )
    own_stats, bn_gain, bn_shift = lax.optimization_barrier((own_stats, bn_gain, bn_shift))
    affine = jnp.stack([bn_gain, bn_shift])
    sent, back, grads_in = lax.optimization_barrier((exchanged(sent, PLANE), back, grads_in))
    stats, conv = lax.optimization_barrier((merged(sent, frames), conv))
    (product,) = call(
        moments_kernel, width, [low, inputs, high, segments, conv, own_stats], [((KERNEL, width), F32)],
        [value_copies, id_copies, column_rows],
    )
    wide = jnp.concatenate([low[: 2 * HALF], inputs, high[: 2 * HALF]])
    plain = jnp.dot(
        window_mask(frame_counts[0], first, frames, frames * devices), wide, preferred_element_type=F32
    )
    stats = gathered(stats, COLUMN)

    swished, act_grad, kept, given, norm = call(
        functools.partial(act_kernel, frames * chips), width,
        [core.reshape(1), low, inputs, high, segments, conv, back, stats, own_stats, affine, plain, product],
        [((frames, width), bf16), ((rows, width), F32), ((chips, 4, width), F32), ((chips, 4, width), F32),
         ((2, width), F32)],
        [value_copies, id_copies, column_rows, pltpu.VMEM((KERNEL, TILE), F32)],
    )
    sent, swished = lax.optimization_barrier((kept + rotated(given, "c", 1), swished))
    sent = exchanged(sent, PLANE)

    share = width // chips
    right_width = half_width // 3
    left_width = half_width - right_width
    height = share + 16
    left, right = pl.pallas_call(
        weight_kernel,
        grid_spec=pltpu.PrefetchScalarGridSpec(
            num_scalar_prefetch=1,
            grid=(4,),
            in_specs=[pl.BlockSpec((frames, width // 4), lambda i, own: (0, i))] * 2
            + [pl.BlockSpec((frames, half_width), lambda i, own: (0, own[0]))] * 2,
            out_specs=[
                pl.BlockSpec((chips // 4, share, left_width), lambda i, own: (i, 0, 0)),
                pl.BlockSpec((chips // 4, height, right_width), lambda i, own: (i, 0, 0)),
            ],
        ),
        out_shape=[
            jax.ShapeDtypeStruct((chips, share, left_width), bf16),
            jax.ShapeDtypeStruct((chips, height, right_width), bf16),
        ],
        compiler_params=PARAMS,
        cost_estimate=pl.CostEstimate(
            flops=4 * frames * width * half_width, bytes_accessed=6 * width * half_width, transcendentals=0
        ),
    )(core.reshape(1), swished, rotated(swished, "c", 1), grads_in, rotated(grads_in, "c", 1))
    block = jnp.dot(swished, proj_weight, preferred_element_type=F32).astype(bf16)
    sent, left, right = lax.optimization_barrier((sent, left, right))
    left = exchanged(left, PLANE)

    sent = jnp.sum(sent, axis=0)
    bit = 1
    while bit < lax.axis_size("z"):
        sent = sent + crossed(sent, "z", bit)
        bit *= 2
    sums = doubled(sent[3:], "c", 1)
    sums, sent, left, right = lax.optimization_barrier((sums, sent, left, right))
    right = pl.pallas_call(
        functools.partial(tap_kernel, total_rows),
        grid=(1,),
        in_specs=[cut(a.shape, 0) for a in (sent, sums, norm, affine)] + [pl.BlockSpec(memory_space=pl.ANY)],
        out_specs=pl.BlockSpec((chips, height - share, right_width), lambda i: (0, share // (height - share), 0)),
        out_shape=jax.ShapeDtypeStruct(right.shape, bf16),
        input_output_aliases={4: 0},
        compiler_params=PARAMS,
    )(sent, sums, norm, affine, right)
    right = exchanged(right, PLANE)

    (frame_grad,) = call(
        functools.partial(frame_kernel, total_rows), width,
        [segments, conv, act_grad, norm, sums, affine, tap_weight], [((frames, width), bf16)],
        [value_copies, id_copies, column_rows],
    )
    right, frame_grad, block = lax.optimization_barrier((right, frame_grad, block))
    part, tap_grad = pl.pallas_call(
        collect_kernel,
        grid=(1,),
        in_specs=[cut(left.shape, 0), cut(right.shape, 0)],
        out_specs=[cut((column, share // column, half_width), 0), cut((chips, width), 0)],
        out_shape=[
            jax.ShapeDtypeStruct((column, share // column, half_width), F32),
            jax.ShapeDtypeStruct((chips, width), F32),
        ],
        compiler_params=PARAMS,
    )(left, right)
    tap_grad = doubled(tap_grad, "c", 1)
    part = exchanged(part, COLUMN)
    part = jnp.sum(part.reshape((2, column // 2) + part.shape[1:]), axis=1)
    proj_grad = jnp.concatenate([part[0], part[1]], axis=1)
    return (block[None], frame_grad[None], tap_grad, sums[1], sums[0], proj_grad)


def solution(mesh):
    grid = Mesh(mesh.devices.reshape(4, 4, 2, -1), ("x", "y", "c", "z"))
    wide = P("z", SEQ, None)
    return jax.shard_map(
        local,
        mesh=grid,
        in_specs=(P("z", None), wide, P(), P(), P(), P(), wide),
        out_specs=(wide, wide, P(), P(), P(), P(("x", "y", "c", "z"), None)),
        check_vma=False,
    )
```

```python
import functools

import jax
import jax.numpy as jnp
from jax import lax
from jax.experimental import pallas as pl
from jax.experimental.pallas import tpu as pltpu
from jax.sharding import Mesh, PartitionSpec as P

HALF = 16
KERNEL = 2 * HALF
EPSILON = 1e-05
SEQ = ("x", "y", "c")
PLANE = ("x", "y")
COLUMN = ("c", "z")
LANES = 128
TILE = 512
SUB = 8
BLOCKS = 4
GROUP = 4
F32 = jnp.float32


def shifted(value, axes, step):
    count = lax.axis_size(axes)
    pairs = [(i, i + step) for i in range(count) if 0 <= i + step < count]
    return lax.ppermute(value, axes, pairs)


def rotated(value, axis, step):
    count = lax.axis_size(axis)
    return lax.ppermute(value, axis, [(i, (i + step) % count) for i in range(count)])


def crossed(value, axis, bit):
    count = lax.axis_size(axis)
    return lax.ppermute(value, axis, [(i, i ^ bit) for i in range(count)])


def doubled(value, axis, bit):
    other = crossed(value, axis, bit)
    upper = (lax.axis_index(axis) & bit) != 0
    first, second = jnp.where(upper, other, value), jnp.where(upper, value, other)
    return jnp.concatenate([first, second])


def exchanged(blocks, axes):
    return lax.all_to_all(blocks, axes, 0, 0, tiled=True)


def gathered(value, axes):
    count = lax.axis_size(axes)
    return exchanged(jnp.broadcast_to(value[None], (count,) + value.shape), axes)


def merged(stats, count):
    means, squares = stats[:, 0], stats[:, 1]
    mean = jnp.mean(means, axis=0)
    spread = jnp.sum(jnp.square(means - mean), axis=0)
    return jnp.stack([mean, jnp.sum(squares, axis=0) + count * spread])


def segment_ids(counts, positions, frames):
    ends = jnp.cumsum(counts)
    found = jnp.sum((positions[:, None] >= ends[None, :]).astype(jnp.int32), axis=1)
    return jnp.where((positions >= 0) & (positions < frames), found, -1)


def window_mask(counts, first, frames, limit):
    row = lax.broadcasted_iota(jnp.int32, (KERNEL, frames + 4 * HALF), 1)
    owner = row + HALF - lax.broadcasted_iota(jnp.int32, row.shape, 0)
    ends = jnp.cumsum(counts)[:, None, None]
    same = jnp.all((first + row >= ends) == (first + owner >= ends), axis=0)
    inside = (owner >= 2 * HALF) & (owner < 2 * HALF + frames)
    valid = (first + row >= 0) & (first + row < limit)
    return (same & inside & valid).astype(jnp.bfloat16)


def shift_copies(source, copies):
    rows = copies.shape[1]
    for b in range(SUB):
        copies[b] = source[b : b + rows]


def lane_groups():
    tiles = [pl.ds(t * LANES, LANES) for t in range(TILE // LANES)]
    return [tiles[t : t + GROUP] for t in range(0, len(tiles), GROUP)]


def convolve(ids_ref, ids, copies, taps_ref, out_ref, rows, centre, tap_of, id_shift):
    offsets = [o for o in range(KERNEL + 1) if 0 <= tap_of(o) < KERNEL]
    for tiles in lane_groups():
        def step(j, carry, tiles=tiles):
            base = pl.multiple_of(j * SUB * BLOCKS, SUB * BLOCKS)
            own = [ids_ref[pl.ds(base + i * SUB + centre, SUB), :] for i in range(BLOCKS)]
            totals = [[jnp.zeros((SUB, LANES), F32) for _ in tiles] for _ in range(BLOCKS)]
            for low in range(SUB):
                steps = [o // SUB for o in offsets if o % SUB == low]
                reads = range(min(steps), max(steps) + BLOCKS)
                near = {i: ids[low, pl.ds(base + i * SUB + id_shift, SUB), :] for i in reads}
                keep = {(a, i): near[a + i] == own[i] for a in steps for i in range(BLOCKS)}
                for t, lanes in enumerate(tiles):
                    value = {i: copies[low, pl.ds(base + i * SUB, SUB), lanes] for i in reads}
                    for a in steps:
                        tap = taps_ref[pl.ds(tap_of(a * SUB + low), 1), lanes]
                        for i in range(BLOCKS):
                            term = jnp.where(keep[a, i], value[a + i], 0.0)
                            totals[i][t] = totals[i][t] + tap * term
            for i in range(BLOCKS):
                for t, lanes in enumerate(tiles):
                    out_ref[pl.ds(base + i * SUB, SUB), lanes] = totals[i][t]
            return carry

        lax.fori_loop(0, rows // (SUB * BLOCKS), step, 0)


def correlate(grad_ref, ids_ref, ids, copies, rows, first, out_ref):
    steps = range(KERNEL // SUB)
    for tiles in lane_groups():
        for low in range(SUB):
            def step(j, sums, tiles=tiles, low=low):
                base = pl.multiple_of(j * SUB * BLOCKS, SUB * BLOCKS)
                reads = range(len(steps) + BLOCKS - 1)
                own = [ids_ref[pl.ds(base + i * SUB + first + HALF, SUB), :] for i in range(BLOCKS)]
                near = [ids[low, pl.ds(base + i * SUB + first, SUB), :] for i in reads]
                keep = {(a, i): near[a + i] == own[i] for a in steps for i in range(BLOCKS)}
                out = list(sums)
                for t, lanes in enumerate(tiles):
                    value = [copies[low, pl.ds(base + i * SUB + first, SUB), lanes] for i in reads]
                    grads = [grad_ref[pl.ds(base + i * SUB, SUB), lanes] for i in range(BLOCKS)]
                    for a in steps:
                        at = t * len(steps) + a
                        for i in range(BLOCKS):
                            out[at] = out[at] + jnp.where(keep[a, i], value[a + i], 0.0) * grads[i]
                return tuple(out)

            start = tuple(jnp.zeros((SUB, LANES), F32) for _ in range(len(steps) * len(tiles)))
            sums = lax.fori_loop(0, rows // (SUB * BLOCKS), step, start)
            for t, lanes in enumerate(tiles):
                for a in steps:
                    total = jnp.sum(sums[t * len(steps) + a], axis=0, keepdims=True)
                    out_ref[pl.ds(a * SUB + low, 1), lanes] = total


def prepare(low_ref, mid_ref, high_ref, ids_ref, copies, ids):
    @pl.when(pl.program_id(0) == 0)
    def _():
        shift_copies(ids_ref[...], ids)

    parts = [low_ref[...][: 2 * HALF], mid_ref[...], high_ref[...][: 2 * HALF]]
    shift_copies(jnp.concatenate([p.astype(F32) for p in parts]), copies)


def conv_kernel(low_ref, mid_ref, high_ref, ids_ref, taps_ref, conv_ref, stats_ref, sent_ref, copies, ids):
    rows = conv_ref.shape[0]
    prepare(low_ref, mid_ref, high_ref, ids_ref, copies, ids)
    convolve(ids_ref, ids, copies, taps_ref, conv_ref, rows, HALF, lambda o: o, 0)
    inner = conv_ref[HALF : rows - HALF, :]
    mean = jnp.sum(inner, axis=0, keepdims=True) / inner.shape[0]
    stats = jnp.concatenate([mean, jnp.sum(jnp.square(inner - mean), axis=0, keepdims=True)])
    stats_ref[...] = stats
    sent_ref[...] = jnp.broadcast_to(stats[None], sent_ref.shape)


def moments_kernel(
    low_ref, mid_ref, high_ref, ids_ref, conv_ref, stats_ref, out_ref, copies, ids, centred
):
    rows = conv_ref.shape[0] - 2 * HALF
    prepare(low_ref, mid_ref, high_ref, ids_ref, copies, ids)
    centred[...] = conv_ref[HALF : HALF + rows, :] - stats_ref[0:1, :]
    correlate(centred, ids_ref, ids, copies, rows, HALF, out_ref)


def act_kernel(
    count, core_ref, low_ref, mid_ref, high_ref, ids_ref, conv_ref, back_ref, all_ref, own_ref, affine_ref,
    plain_ref, product_ref, swished_ref, grad_ref, kept_ref, given_ref, norm_ref, copies, ids, centred, taps,
):
    rows = conv_ref.shape[0] - 2 * HALF
    prepare(low_ref, mid_ref, high_ref, ids_ref, copies, ids)
    merge = all_ref.shape[0]
    means = [all_ref[i, 0:1, :] for i in range(merge)]
    mean = sum(means) / merge
    spread = sum(jnp.square(m - mean) for m in means)
    var = (sum(all_ref[i, 1:2, :] for i in range(merge)) + count * spread) / (count * merge)
    inverse = lax.rsqrt(var + EPSILON)
    norm_ref[...] = jnp.concatenate([mean, inverse])
    normed = (conv_ref[...] - mean) * inverse
    act = affine_ref[0:1, :] * normed + affine_ref[1:2, :]
    gate = jax.nn.sigmoid(act)
    grad = back_ref[...] * gate * (1.0 + act * (1.0 - gate))
    grad_ref[...] = grad
    swished_ref[...] = (act * gate)[HALF : HALF + rows].astype(jnp.bfloat16)
    inner, inner_normed = grad[HALF : HALF + rows], normed[HALF : HALF + rows]
    sums = [jnp.sum(inner, axis=0, keepdims=True), jnp.sum(inner * inner_normed, axis=0, keepdims=True)]
    centred[...] = inner
    correlate(centred, ids_ref, ids, copies, rows, HALF, taps)
    plain = plain_ref[...]
    product = inverse * (product_ref[...] + (own_ref[0:1, :] - mean) * plain)
    chips = kept_ref.shape[0]
    first = core_ref[0] == 0
    for i in range(chips):
        low, high = (
            jnp.concatenate([v[at : at + 1] for v in (taps, plain, product)] + [sums[at // chips]])
            for at in (i, chips + i)
        )
        kept_ref[i] = jnp.where(first, low, high)
        given_ref[i] = jnp.where(first, high, low)


def weight_kernel(_, own_ref, other_ref, own_grad_ref, other_grad_ref, left_ref, right_ref):
    over = (((0,), (0,)), ((), ()))
    part = lax.dot_general(own_ref[...], own_grad_ref[...], over, preferred_element_type=F32)
    part = part + lax.dot_general(other_ref[...], other_grad_ref[...], over, preferred_element_type=F32)
    part = part.astype(jnp.bfloat16)
    each, left = left_ref.shape[1:]
    for i in range(left_ref.shape[0]):
        left_ref[i] = part[i * each : (i + 1) * each, :left]
        right_ref[i, 0:each, :] = part[i * each : (i + 1) * each, left:]


def tap_kernel(total_rows, parts_ref, sums_ref, norm_ref, affine_ref, _, out_ref):
    scale = affine_ref[0:1, :] * norm_ref[1:2, :]
    shift, slope = sums_ref[0:1, :] / total_rows, sums_ref[1:2, :] / total_rows
    rest = scale * (parts_ref[0:1, :] - shift * parts_ref[1:2, :] - slope * parts_ref[2:3, :])
    height, size = out_ref.shape[1:]
    rows = []
    for _ in range(2):
        term = rest.astype(jnp.bfloat16).astype(F32)
        rows += [term[:, at : at + size] for at in range(0, rest.shape[1], size)]
        rest = rest - term
    rows.append(jnp.zeros((height - len(rows), size), F32))
    rows = jnp.concatenate(rows).astype(jnp.bfloat16)
    for i in range(out_ref.shape[0]):
        out_ref[i] = rows


def collect_kernel(left_ref, right_ref, out_ref, taps_ref):
    each = out_ref.shape[1]
    rows, left = left_ref.shape[1:]
    size = right_ref.shape[2]
    for all_ref, columns in ((left_ref, slice(0, left)), (right_ref, slice(left, left + size))):
        total = sum(all_ref[i, 0:rows, :].astype(F32) for i in range(all_ref.shape[0]))
        for i in range(out_ref.shape[0]):
            out_ref[i, :, columns] = total[i * each : (i + 1) * each].astype(out_ref.dtype)
    pieces = taps_ref.shape[1] // size
    for i in range(right_ref.shape[0]):
        terms = right_ref[i, rows:, :].astype(F32)
        terms = terms[:pieces] + terms[pieces : 2 * pieces]
        for piece in range(pieces):
            taps_ref[i : i + 1, piece * size : (piece + 1) * size] = terms[piece : piece + 1]


def frame_kernel(
    total_rows, ids_ref, conv_ref, grad_ref, norm_ref, sums_ref, affine_ref, taps_ref, out_ref, copies, ids, result
):
    rows = out_ref.shape[0]

    @pl.when(pl.program_id(0) == 0)
    def _():
        shift_copies(ids_ref[...], ids)

    mean, inverse = norm_ref[0:1, :], norm_ref[1:2, :]
    scale = affine_ref[0:1, :] * inverse
    shift, slope = sums_ref[0:1, :] / total_rows, sums_ref[1:2, :] / total_rows
    normed = (conv_ref[...] - mean) * inverse
    grad = scale * (grad_ref[...] - shift - normed * slope)
    for b in range(SUB):
        count = rows + 2 * HALF - (SUB if b else 0)
        copies[b, 0:count, :] = grad[b : b + count]

    convolve(
        ids_ref, ids, copies, taps_ref, result, rows, 2 * HALF, lambda o: KERNEL - o, HALF
    )
    out_ref[...] = result[...].astype(jnp.bfloat16)


PARAMS = pltpu.CompilerParams(vmem_limit_bytes=16 * 1024 * 1024)


def cut(shape, width):
    lead = (0,) * (len(shape) - 1)
    if shape == (1,):
        return pl.BlockSpec(memory_space=pltpu.SMEM)
    if shape[-1] != width:
        return pl.BlockSpec(shape, lambda i: lead + (0,))
    return pl.BlockSpec(shape[:-1] + (TILE,), lambda i: lead + (i,))


def call(kernel, width, ins, outs, scratch, weight=1):
    return pl.pallas_call(
        kernel,
        grid=(width // TILE,),
        in_specs=[cut(a.shape, width) for a in ins],
        out_specs=[cut(shape, width) for shape, _ in outs],
        out_shape=[jax.ShapeDtypeStruct(shape, kind) for shape, kind in outs],
        scratch_shapes=scratch,
        compiler_params=PARAMS,
        cost_estimate=pl.CostEstimate(
            flops=weight * 192 * KERNEL * width * 4, bytes_accessed=4 * 224 * width * 4, transcendentals=0
        ),
    )(*ins)


def local(frame_counts, glu_out, tap_weight, bn_gain, bn_shift, proj_weight, out_grad):
    inputs = glu_out[0]
    grads_in = out_grad[0]
    frames, width = inputs.shape
    half_width = width // 2
    devices = lax.axis_size(SEQ)
    chips, column = lax.axis_size(PLANE), lax.axis_size(COLUMN)
    total_rows = frames * chips * column
    core = lax.axis_index("c")
    rows = frames + 2 * HALF
    reach = frames + 4 * HALF - SUB
    bf16 = jnp.bfloat16

    up = jnp.concatenate([inputs[-2 * HALF :], grads_in[-HALF:]])
    down = jnp.concatenate([inputs[: 2 * HALF], grads_in[:HALF]])
    low, high = shifted(up, SEQ, 1), shifted(down, SEQ, -1)
    grads_wide = jnp.concatenate([low[2 * HALF :], grads_in, high[2 * HALF :]])

    first = lax.axis_index(SEQ) * frames - 2 * HALF
    positions = first + jnp.arange(frames + 4 * HALF, dtype=jnp.int32)
    segments = segment_ids(frame_counts[0], positions, frames * devices)
    segments = jnp.broadcast_to(segments[:, None], (frames + 4 * HALF, LANES))
    value_copies = pltpu.VMEM((SUB, reach, TILE), F32)
    id_copies = pltpu.VMEM((SUB, reach, LANES), jnp.int32)
    column_rows = pltpu.VMEM((frames, TILE), F32)

    conv, own_stats, sent = call(
        conv_kernel, width, [low, inputs, high, segments, tap_weight],
        [((rows, width), F32), ((2, width), F32), ((chips, 2, width), F32)],
        [value_copies, id_copies],
    )
    back = lax.dot_general(
        grads_wide, proj_weight, (((1,), (1,)), ((), ())), preferred_element_type=F32
    )
    own_stats, bn_gain, bn_shift = lax.optimization_barrier((own_stats, bn_gain, bn_shift))
    affine = jnp.stack([bn_gain, bn_shift])
    sent, back, grads_in = lax.optimization_barrier((exchanged(sent, PLANE), back, grads_in))
    stats, conv = lax.optimization_barrier((merged(sent, frames), conv))
    (product,) = call(
        moments_kernel, width, [low, inputs, high, segments, conv, own_stats], [((KERNEL, width), F32)],
        [value_copies, id_copies, column_rows],
    )
    wide = jnp.concatenate([low[: 2 * HALF], inputs, high[: 2 * HALF]])
    plain = jnp.dot(
        window_mask(frame_counts[0], first, frames, frames * devices), wide, preferred_element_type=F32
    )
    stats = gathered(stats, COLUMN)

    swished, act_grad, kept, given, norm = call(
        functools.partial(act_kernel, frames * chips), width,
        [core.reshape(1), low, inputs, high, segments, conv, back, stats, own_stats, affine, plain, product],
        [((frames, width), bf16), ((rows, width), F32), ((chips, 4, width), F32), ((chips, 4, width), F32),
         ((2, width), F32)],
        [value_copies, id_copies, column_rows, pltpu.VMEM((KERNEL, TILE), F32)],
    )
    sent, swished = lax.optimization_barrier((kept + rotated(given, "c", 1), swished))
    sent = exchanged(sent, PLANE)

    share = width // chips
    right_width = half_width // 3
    left_width = half_width - right_width
    height = share + 16
    left, right = pl.pallas_call(
        weight_kernel,
        grid_spec=pltpu.PrefetchScalarGridSpec(
            num_scalar_prefetch=1,
            grid=(4,),
            in_specs=[pl.BlockSpec((frames, width // 4), lambda i, own: (0, i))] * 2
            + [pl.BlockSpec((frames, half_width), lambda i, own: (0, own[0]))] * 2,
            out_specs=[
                pl.BlockSpec((chips // 4, share, left_width), lambda i, own: (i, 0, 0)),
                pl.BlockSpec((chips // 4, height, right_width), lambda i, own: (i, 0, 0)),
            ],
        ),
        out_shape=[
            jax.ShapeDtypeStruct((chips, share, left_width), bf16),
            jax.ShapeDtypeStruct((chips, height, right_width), bf16),
        ],
        compiler_params=PARAMS,
        cost_estimate=pl.CostEstimate(
            flops=4 * frames * width * half_width, bytes_accessed=6 * width * half_width, transcendentals=0
        ),
    )(core.reshape(1), swished, rotated(swished, "c", 1), grads_in, rotated(grads_in, "c", 1))
    block = jnp.dot(swished, proj_weight, preferred_element_type=F32).astype(bf16)
    sent, left, right = lax.optimization_barrier((sent, left, right))
    left = exchanged(left, PLANE)

    sent = jnp.sum(sent, axis=0)
    bit = 1
    while bit < lax.axis_size("z"):
        sent = sent + crossed(sent, "z", bit)
        bit *= 2
    sums = doubled(sent[3:], "c", 1)
    sums, sent, left, right = lax.optimization_barrier((sums, sent, left, right))
    right = pl.pallas_call(
        functools.partial(tap_kernel, total_rows),
        grid=(1,),
        in_specs=[cut(a.shape, 0) for a in (sent, sums, norm, affine)] + [pl.BlockSpec(memory_space=pl.ANY)],
        out_specs=pl.BlockSpec((chips, height - share, right_width), lambda i: (0, share // (height - share), 0)),
        out_shape=jax.ShapeDtypeStruct(right.shape, bf16),
        input_output_aliases={4: 0},
        compiler_params=PARAMS,
    )(sent, sums, norm, affine, right)
    right = exchanged(right, PLANE)

    (frame_grad,) = call(
        functools.partial(frame_kernel, total_rows), width,
        [segments, conv, act_grad, norm, sums, affine, tap_weight], [((frames, width), bf16)],
        [value_copies, id_copies, column_rows],
    )
    right, frame_grad, block = lax.optimization_barrier((right, frame_grad, block))
    part, tap_grad = pl.pallas_call(
        collect_kernel,
        grid=(1,),
        in_specs=[cut(left.shape, 0), cut(right.shape, 0)],
        out_specs=[cut((column, share // column, half_width), 0), cut((chips, width), 0)],
        out_shape=[
            jax.ShapeDtypeStruct((column, share // column, half_width), bf16),
            jax.ShapeDtypeStruct((chips, width), F32),
        ],
        compiler_params=PARAMS,
    )(left, right)
    tap_grad = doubled(tap_grad, "c", 1)
    part = exchanged(part, COLUMN).astype(F32)
    part = jnp.sum(part.reshape((2, column // 2) + part.shape[1:]), axis=1)
    proj_grad = jnp.concatenate([part[0], part[1]], axis=1)
    return (block[None], frame_grad[None], tap_grad, sums[1], sums[0], proj_grad)


def solution(mesh):
    grid = Mesh(mesh.devices.reshape(4, 4, 2, -1), ("x", "y", "c", "z"))
    wide = P("z", SEQ, None)
    return jax.shard_map(
        local,
        mesh=grid,
        in_specs=(P("z", None), wide, P(), P(), P(), P(), wide),
        out_specs=(wide, wide, P(), P(), P(), P(("x", "y", "c", "z"), None)),
        check_vma=False,
    )
```

```python
import functools

import jax
import jax.numpy as jnp
from jax import lax
from jax.experimental import pallas as pl
from jax.experimental.pallas import tpu as pltpu
from jax.sharding import Mesh, PartitionSpec as P

HALF = 16
KERNEL = 2 * HALF
EPSILON = 1e-05
SEQ = ("x", "y", "c")
PLANE = ("x", "y")
COLUMN = ("c", "z")
LANES = 128
TILE = 512
SUB = 8
WIDEST = 8
GROUP = 4
F32 = jnp.float32


def shifted(value, axes, step):
    count = lax.axis_size(axes)
    pairs = [(i, i + step) for i in range(count) if 0 <= i + step < count]
    return lax.ppermute(value, axes, pairs)


def rotated(value, axis, step):
    count = lax.axis_size(axis)
    return lax.ppermute(value, axis, [(i, (i + step) % count) for i in range(count)])


def crossed(value, axis, bit):
    count = lax.axis_size(axis)
    return lax.ppermute(value, axis, [(i, i ^ bit) for i in range(count)])


def doubled(value, axis, bit):
    other = crossed(value, axis, bit)
    upper = (lax.axis_index(axis) & bit) != 0
    first, second = jnp.where(upper, other, value), jnp.where(upper, value, other)
    return jnp.concatenate([first, second])


def exchanged(blocks, axes):
    return lax.all_to_all(blocks, axes, 0, 0, tiled=True)


def gathered(value, axes):
    count = lax.axis_size(axes)
    return exchanged(jnp.broadcast_to(value[None], (count,) + value.shape), axes)


def merged(stats, count):
    means, squares = stats[:, 0], stats[:, 1]
    mean = jnp.mean(means, axis=0)
    spread = jnp.sum(jnp.square(means - mean), axis=0)
    return jnp.stack([mean, jnp.sum(squares, axis=0) + count * spread])


def segment_ids(counts, positions, frames):
    ends = jnp.cumsum(counts)
    found = jnp.sum((positions[:, None] >= ends[None, :]).astype(jnp.int32), axis=1)
    return jnp.where((positions >= 0) & (positions < frames), found, -1)


def window_mask(counts, first, frames, limit):
    row = lax.broadcasted_iota(jnp.int32, (KERNEL, frames + 4 * HALF), 1)
    owner = row + HALF - lax.broadcasted_iota(jnp.int32, row.shape, 0)
    ends = jnp.cumsum(counts)[:, None, None]
    same = jnp.all((first + row >= ends) == (first + owner >= ends), axis=0)
    inside = (owner >= 2 * HALF) & (owner < 2 * HALF + frames)
    valid = (first + row >= 0) & (first + row < limit)
    return (same & inside & valid).astype(jnp.bfloat16)


def shift_copies(source, copies):
    rows = copies.shape[1]
    for b in range(SUB):
        copies[b] = source[b : b + rows]


def lane_groups():
    tiles = [pl.ds(t * LANES, LANES) for t in range(TILE // LANES)]
    return [tiles[t : t + GROUP] for t in range(0, len(tiles), GROUP)]


def blocks_of(rows):
    count = rows // SUB
    return max(b for b in range(1, WIDEST + 1) if count % b == 0)


def convolve(ids_ref, ids, copies, taps_ref, out_ref, rows, centre, tap_of, id_shift):
    blocks = blocks_of(rows)
    offsets = [o for o in range(KERNEL + 1) if 0 <= tap_of(o) < KERNEL]
    for tiles in lane_groups():
        def step(j, carry, tiles=tiles):
            base = pl.multiple_of(j * SUB * blocks, SUB * blocks)
            own = [ids_ref[pl.ds(base + i * SUB + centre, SUB), :] for i in range(blocks)]
            totals = [[jnp.zeros((SUB, LANES), F32) for _ in tiles] for _ in range(blocks)]
            for low in range(SUB):
                steps = [o // SUB for o in offsets if o % SUB == low]
                reads = range(min(steps), max(steps) + blocks)
                near = {i: ids[low, pl.ds(base + i * SUB + id_shift, SUB), :] for i in reads}
                keep = {(a, i): near[a + i] == own[i] for a in steps for i in range(blocks)}
                for t, lanes in enumerate(tiles):
                    value = {i: copies[low, pl.ds(base + i * SUB, SUB), lanes] for i in reads}
                    for a in steps:
                        tap = taps_ref[pl.ds(tap_of(a * SUB + low), 1), lanes]
                        for i in range(blocks):
                            term = jnp.where(keep[a, i], value[a + i], 0.0)
                            totals[i][t] = totals[i][t] + tap * term
            for i in range(blocks):
                for t, lanes in enumerate(tiles):
                    out_ref[pl.ds(base + i * SUB, SUB), lanes] = totals[i][t]
            return carry

        lax.fori_loop(0, rows // (SUB * blocks), step, 0)


def correlate(grad_ref, ids_ref, ids, copies, rows, first, out_ref):
    blocks = blocks_of(rows)
    steps = range(KERNEL // SUB)
    for tiles in lane_groups():
        for low in range(SUB):
            def step(j, sums, tiles=tiles, low=low):
                base = pl.multiple_of(j * SUB * blocks, SUB * blocks)
                reads = range(len(steps) + blocks - 1)
                own = [ids_ref[pl.ds(base + i * SUB + first + HALF, SUB), :] for i in range(blocks)]
                near = [ids[low, pl.ds(base + i * SUB + first, SUB), :] for i in reads]
                keep = {(a, i): near[a + i] == own[i] for a in steps for i in range(blocks)}
                out = list(sums)
                for t, lanes in enumerate(tiles):
                    value = [copies[low, pl.ds(base + i * SUB + first, SUB), lanes] for i in reads]
                    grads = [grad_ref[pl.ds(base + i * SUB, SUB), lanes] for i in range(blocks)]
                    for a in steps:
                        at = t * len(steps) + a
                        for i in range(blocks):
                            out[at] = out[at] + jnp.where(keep[a, i], value[a + i], 0.0) * grads[i]
                return tuple(out)

            start = tuple(jnp.zeros((SUB, LANES), F32) for _ in range(len(steps) * len(tiles)))
            sums = lax.fori_loop(0, rows // (SUB * blocks), step, start)
            for t, lanes in enumerate(tiles):
                for a in steps:
                    total = jnp.sum(sums[t * len(steps) + a], axis=0, keepdims=True)
                    out_ref[pl.ds(a * SUB + low, 1), lanes] = total


def prepare(low_ref, mid_ref, high_ref, ids_ref, copies, ids):
    @pl.when(pl.program_id(0) == 0)
    def _():
        shift_copies(ids_ref[...], ids)

    parts = [low_ref[...][: 2 * HALF], mid_ref[...], high_ref[...][: 2 * HALF]]
    shift_copies(jnp.concatenate([p.astype(F32) for p in parts]), copies)


def conv_kernel(low_ref, mid_ref, high_ref, ids_ref, taps_ref, conv_ref, stats_ref, sent_ref, copies, ids):
    rows = conv_ref.shape[0]
    prepare(low_ref, mid_ref, high_ref, ids_ref, copies, ids)
    convolve(ids_ref, ids, copies, taps_ref, conv_ref, rows, HALF, lambda o: o, 0)
    inner = conv_ref[HALF : rows - HALF, :]
    mean = jnp.sum(inner, axis=0, keepdims=True) / inner.shape[0]
    stats = jnp.concatenate([mean, jnp.sum(jnp.square(inner - mean), axis=0, keepdims=True)])
    stats_ref[...] = stats
    sent_ref[...] = jnp.broadcast_to(stats[None], sent_ref.shape)


def moments_kernel(
    low_ref, mid_ref, high_ref, ids_ref, conv_ref, stats_ref, out_ref, copies, ids, centred
):
    rows = conv_ref.shape[0] - 2 * HALF
    prepare(low_ref, mid_ref, high_ref, ids_ref, copies, ids)
    centred[...] = conv_ref[HALF : HALF + rows, :] - stats_ref[0:1, :]
    correlate(centred, ids_ref, ids, copies, rows, HALF, out_ref)


def act_kernel(
    count, core_ref, low_ref, mid_ref, high_ref, ids_ref, conv_ref, back_ref, all_ref, own_ref, affine_ref,
    plain_ref, product_ref, swished_ref, grad_ref, kept_ref, given_ref, norm_ref, copies, ids, centred, taps,
):
    rows = conv_ref.shape[0] - 2 * HALF
    prepare(low_ref, mid_ref, high_ref, ids_ref, copies, ids)
    merge = all_ref.shape[0]
    means = [all_ref[i, 0:1, :] for i in range(merge)]
    mean = sum(means) / merge
    spread = sum(jnp.square(m - mean) for m in means)
    var = (sum(all_ref[i, 1:2, :] for i in range(merge)) + count * spread) / (count * merge)
    inverse = lax.rsqrt(var + EPSILON)
    norm_ref[...] = jnp.concatenate([mean, inverse])
    normed = (conv_ref[...] - mean) * inverse
    act = affine_ref[0:1, :] * normed + affine_ref[1:2, :]
    gate = jax.nn.sigmoid(act)
    grad = back_ref[...] * gate * (1.0 + act * (1.0 - gate))
    grad_ref[...] = grad
    swished_ref[...] = (act * gate)[HALF : HALF + rows].astype(jnp.bfloat16)
    inner, inner_normed = grad[HALF : HALF + rows], normed[HALF : HALF + rows]
    sums = [jnp.sum(inner, axis=0, keepdims=True), jnp.sum(inner * inner_normed, axis=0, keepdims=True)]
    centred[...] = inner
    correlate(centred, ids_ref, ids, copies, rows, HALF, taps)
    plain = plain_ref[...]
    product = inverse * (product_ref[...] + (own_ref[0:1, :] - mean) * plain)
    chips = kept_ref.shape[0]
    first = core_ref[0] == 0
    for i in range(chips):
        low, high = (
            jnp.concatenate([v[at : at + 1] for v in (taps, plain, product)] + [sums[at // chips]])
            for at in (i, chips + i)
        )
        kept_ref[i] = jnp.where(first, low, high)
        given_ref[i] = jnp.where(first, high, low)


def weight_kernel(_, own_ref, other_ref, own_grad_ref, other_grad_ref, left_ref, right_ref):
    over = (((0,), (0,)), ((), ()))
    part = lax.dot_general(own_ref[...], own_grad_ref[...], over, preferred_element_type=F32)
    part = part + lax.dot_general(other_ref[...], other_grad_ref[...], over, preferred_element_type=F32)
    part = part.astype(jnp.bfloat16)
    each, left = left_ref.shape[1:]
    for i in range(left_ref.shape[0]):
        left_ref[i] = part[i * each : (i + 1) * each, :left]
        right_ref[i, 0:each, :] = part[i * each : (i + 1) * each, left:]


def tap_kernel(total_rows, parts_ref, sums_ref, norm_ref, affine_ref, _, out_ref):
    scale = affine_ref[0:1, :] * norm_ref[1:2, :]
    shift, slope = sums_ref[0:1, :] / total_rows, sums_ref[1:2, :] / total_rows
    rest = scale * (parts_ref[0:1, :] - shift * parts_ref[1:2, :] - slope * parts_ref[2:3, :])
    height, size = out_ref.shape[1:]
    rows = []
    for _ in range(2):
        term = rest.astype(jnp.bfloat16).astype(F32)
        rows += [term[:, at : at + size] for at in range(0, rest.shape[1], size)]
        rest = rest - term
    rows.append(jnp.zeros((height - len(rows), size), F32))
    rows = jnp.concatenate(rows).astype(jnp.bfloat16)
    for i in range(out_ref.shape[0]):
        out_ref[i] = rows


def collect_kernel(left_ref, right_ref, out_ref, taps_ref):
    each = out_ref.shape[1]
    rows, left = left_ref.shape[1:]
    size = right_ref.shape[2]
    for all_ref, columns in ((left_ref, slice(0, left)), (right_ref, slice(left, left + size))):
        total = sum(all_ref[i, 0:rows, :].astype(F32) for i in range(all_ref.shape[0]))
        for i in range(out_ref.shape[0]):
            out_ref[i, :, columns] = total[i * each : (i + 1) * each].astype(out_ref.dtype)
    pieces = taps_ref.shape[1] // size
    for i in range(right_ref.shape[0]):
        terms = right_ref[i, rows:, :].astype(F32)
        terms = terms[:pieces] + terms[pieces : 2 * pieces]
        for piece in range(pieces):
            taps_ref[i : i + 1, piece * size : (piece + 1) * size] = terms[piece : piece + 1]


def frame_kernel(
    total_rows, ids_ref, conv_ref, grad_ref, norm_ref, sums_ref, affine_ref, taps_ref, out_ref, copies, ids, result
):
    rows = out_ref.shape[0]

    @pl.when(pl.program_id(0) == 0)
    def _():
        shift_copies(ids_ref[...], ids)

    mean, inverse = norm_ref[0:1, :], norm_ref[1:2, :]
    scale = affine_ref[0:1, :] * inverse
    shift, slope = sums_ref[0:1, :] / total_rows, sums_ref[1:2, :] / total_rows
    normed = (conv_ref[...] - mean) * inverse
    grad = scale * (grad_ref[...] - shift - normed * slope)
    for b in range(SUB):
        count = rows + 2 * HALF - (SUB if b else 0)
        copies[b, 0:count, :] = grad[b : b + count]

    convolve(
        ids_ref, ids, copies, taps_ref, result, rows, 2 * HALF, lambda o: KERNEL - o, HALF
    )
    out_ref[...] = result[...].astype(jnp.bfloat16)


PARAMS = pltpu.CompilerParams(vmem_limit_bytes=16 * 1024 * 1024)


def cut(shape, width):
    lead = (0,) * (len(shape) - 1)
    if shape == (1,):
        return pl.BlockSpec(memory_space=pltpu.SMEM)
    if shape[-1] != width:
        return pl.BlockSpec(shape, lambda i: lead + (0,))
    return pl.BlockSpec(shape[:-1] + (TILE,), lambda i: lead + (i,))


def call(kernel, width, ins, outs, scratch, weight=1):
    return pl.pallas_call(
        kernel,
        grid=(width // TILE,),
        in_specs=[cut(a.shape, width) for a in ins],
        out_specs=[cut(shape, width) for shape, _ in outs],
        out_shape=[jax.ShapeDtypeStruct(shape, kind) for shape, kind in outs],
        scratch_shapes=scratch,
        compiler_params=PARAMS,
        cost_estimate=pl.CostEstimate(
            flops=weight * 192 * KERNEL * width * 4, bytes_accessed=4 * 224 * width * 4, transcendentals=0
        ),
    )(*ins)


def local(frame_counts, glu_out, tap_weight, bn_gain, bn_shift, proj_weight, out_grad):
    inputs = glu_out[0]
    grads_in = out_grad[0]
    frames, width = inputs.shape
    half_width = width // 2
    devices = lax.axis_size(SEQ)
    chips, column = lax.axis_size(PLANE), lax.axis_size(COLUMN)
    total_rows = frames * chips * column
    core = lax.axis_index("c")
    rows = frames + 2 * HALF
    reach = frames + 4 * HALF - SUB
    bf16 = jnp.bfloat16

    up = jnp.concatenate([inputs[-2 * HALF :], grads_in[-HALF:]])
    down = jnp.concatenate([inputs[: 2 * HALF], grads_in[:HALF]])
    low, high = shifted(up, SEQ, 1), shifted(down, SEQ, -1)
    grads_wide = jnp.concatenate([low[2 * HALF :], grads_in, high[2 * HALF :]])

    first = lax.axis_index(SEQ) * frames - 2 * HALF
    positions = first + jnp.arange(frames + 4 * HALF, dtype=jnp.int32)
    segments = segment_ids(frame_counts[0], positions, frames * devices)
    segments = jnp.broadcast_to(segments[:, None], (frames + 4 * HALF, LANES))
    value_copies = pltpu.VMEM((SUB, reach, TILE), F32)
    id_copies = pltpu.VMEM((SUB, reach, LANES), jnp.int32)
    column_rows = pltpu.VMEM((frames, TILE), F32)

    conv, own_stats, sent = call(
        conv_kernel, width, [low, inputs, high, segments, tap_weight],
        [((rows, width), F32), ((2, width), F32), ((chips, 2, width), F32)],
        [value_copies, id_copies],
    )
    back = lax.dot_general(
        grads_wide, proj_weight, (((1,), (1,)), ((), ())), preferred_element_type=F32
    )
    own_stats, bn_gain, bn_shift = lax.optimization_barrier((own_stats, bn_gain, bn_shift))
    affine = jnp.stack([bn_gain, bn_shift])
    sent, back, grads_in = lax.optimization_barrier((exchanged(sent, PLANE), back, grads_in))
    stats, conv = lax.optimization_barrier((merged(sent, frames), conv))
    (product,) = call(
        moments_kernel, width, [low, inputs, high, segments, conv, own_stats], [((KERNEL, width), F32)],
        [value_copies, id_copies, column_rows],
    )
    wide = jnp.concatenate([low[: 2 * HALF], inputs, high[: 2 * HALF]])
    plain = jnp.dot(
        window_mask(frame_counts[0], first, frames, frames * devices), wide, preferred_element_type=F32
    )
    stats = gathered(stats, COLUMN)

    swished, act_grad, kept, given, norm = call(
        functools.partial(act_kernel, frames * chips), width,
        [core.reshape(1), low, inputs, high, segments, conv, back, stats, own_stats, affine, plain, product],
        [((frames, width), bf16), ((rows, width), F32), ((chips, 4, width), F32), ((chips, 4, width), F32),
         ((2, width), F32)],
        [value_copies, id_copies, column_rows, pltpu.VMEM((KERNEL, TILE), F32)],
    )
    sent, swished = lax.optimization_barrier((kept + rotated(given, "c", 1), swished))
    sent = exchanged(sent, PLANE)

    share = width // chips
    right_width = half_width // 3
    left_width = half_width - right_width
    height = share + 16
    left, right = pl.pallas_call(
        weight_kernel,
        grid_spec=pltpu.PrefetchScalarGridSpec(
            num_scalar_prefetch=1,
            grid=(4,),
            in_specs=[pl.BlockSpec((frames, width // 4), lambda i, own: (0, i))] * 2
            + [pl.BlockSpec((frames, half_width), lambda i, own: (0, own[0]))] * 2,
            out_specs=[
                pl.BlockSpec((chips // 4, share, left_width), lambda i, own: (i, 0, 0)),
                pl.BlockSpec((chips // 4, height, right_width), lambda i, own: (i, 0, 0)),
            ],
        ),
        out_shape=[
            jax.ShapeDtypeStruct((chips, share, left_width), bf16),
            jax.ShapeDtypeStruct((chips, height, right_width), bf16),
        ],
        compiler_params=PARAMS,
        cost_estimate=pl.CostEstimate(
            flops=4 * frames * width * half_width, bytes_accessed=6 * width * half_width, transcendentals=0
        ),
    )(core.reshape(1), swished, rotated(swished, "c", 1), grads_in, rotated(grads_in, "c", 1))
    block = jnp.dot(swished, proj_weight, preferred_element_type=F32).astype(bf16)
    sent, left, right = lax.optimization_barrier((sent, left, right))
    left = exchanged(left, PLANE)

    sent = jnp.sum(sent, axis=0)
    bit = 1
    while bit < lax.axis_size("z"):
        sent = sent + crossed(sent, "z", bit)
        bit *= 2
    sums = doubled(sent[3:], "c", 1)
    sums, sent, left, right = lax.optimization_barrier((sums, sent, left, right))
    right = pl.pallas_call(
        functools.partial(tap_kernel, total_rows),
        grid=(1,),
        in_specs=[cut(a.shape, 0) for a in (sent, sums, norm, affine)] + [pl.BlockSpec(memory_space=pl.ANY)],
        out_specs=pl.BlockSpec((chips, height - share, right_width), lambda i: (0, share // (height - share), 0)),
        out_shape=jax.ShapeDtypeStruct(right.shape, bf16),
        input_output_aliases={4: 0},
        compiler_params=PARAMS,
    )(sent, sums, norm, affine, right)
    right = exchanged(right, PLANE)

    (frame_grad,) = call(
        functools.partial(frame_kernel, total_rows), width,
        [segments, conv, act_grad, norm, sums, affine, tap_weight], [((frames, width), bf16)],
        [value_copies, id_copies, column_rows],
    )
    right, frame_grad, block = lax.optimization_barrier((right, frame_grad, block))
    part, tap_grad = pl.pallas_call(
        collect_kernel,
        grid=(1,),
        in_specs=[cut(left.shape, 0), cut(right.shape, 0)],
        out_specs=[cut((column, share // column, half_width), 0), cut((chips, width), 0)],
        out_shape=[
            jax.ShapeDtypeStruct((column, share // column, half_width), bf16),
            jax.ShapeDtypeStruct((chips, width), F32),
        ],
        compiler_params=PARAMS,
    )(left, right)
    tap_grad = doubled(tap_grad, "c", 1)
    part = exchanged(part, COLUMN).astype(F32)
    part = jnp.sum(part.reshape((2, column // 2) + part.shape[1:]), axis=1)
    proj_grad = jnp.concatenate([part[0], part[1]], axis=1)
    return (block[None], frame_grad[None], tap_grad, sums[1], sums[0], proj_grad)


def solution(mesh):
    grid = Mesh(mesh.devices.reshape(4, 4, 2, -1), ("x", "y", "c", "z"))
    wide = P("z", SEQ, None)
    return jax.shard_map(
        local,
        mesh=grid,
        in_specs=(P("z", None), wide, P(), P(), P(), P(), wide),
        out_specs=(wide, wide, P(), P(), P(), P(("x", "y", "c", "z"), None)),
        check_vma=False,
    )
```

```python
import functools

import jax
import jax.numpy as jnp
from jax import lax
from jax.experimental import pallas as pl
from jax.experimental.pallas import tpu as pltpu
from jax.sharding import Mesh, PartitionSpec as P

HALF = 16
KERNEL = 2 * HALF
EPSILON = 1e-05
SEQ = ("x", "y", "c")
PLANE = ("x", "y")
COLUMN = ("c", "z")
LANES = 128
TILE = 512
SUB = 8
BLOCKS = 4
GROUP = 4
F32 = jnp.float32


def shifted(value, axes, step):
    count = lax.axis_size(axes)
    pairs = [(i, i + step) for i in range(count) if 0 <= i + step < count]
    return lax.ppermute(value, axes, pairs)


def rotated(value, axis, step):
    count = lax.axis_size(axis)
    return lax.ppermute(value, axis, [(i, (i + step) % count) for i in range(count)])


def crossed(value, axis, bit):
    count = lax.axis_size(axis)
    return lax.ppermute(value, axis, [(i, i ^ bit) for i in range(count)])


def doubled(value, axis, bit):
    other = crossed(value, axis, bit)
    upper = (lax.axis_index(axis) & bit) != 0
    first, second = jnp.where(upper, other, value), jnp.where(upper, value, other)
    return jnp.concatenate([first, second])


def exchanged(blocks, axes):
    return lax.all_to_all(blocks, axes, 0, 0, tiled=True)


def gathered(value, axes):
    count = lax.axis_size(axes)
    return exchanged(jnp.broadcast_to(value[None], (count,) + value.shape), axes)


def merged(stats, count):
    means, squares = stats[:, 0], stats[:, 1]
    mean = jnp.mean(means, axis=0)
    spread = jnp.sum(jnp.square(means - mean), axis=0)
    return jnp.stack([mean, jnp.sum(squares, axis=0) + count * spread])


def segment_ids(counts, positions, frames):
    ends = jnp.cumsum(counts)
    found = jnp.sum((positions[:, None] >= ends[None, :]).astype(jnp.int32), axis=1)
    return jnp.where((positions >= 0) & (positions < frames), found, -1)


def window_mask(counts, first, frames, limit):
    row = lax.broadcasted_iota(jnp.int32, (KERNEL, frames + 4 * HALF), 1)
    owner = row + HALF - lax.broadcasted_iota(jnp.int32, row.shape, 0)
    ends = jnp.cumsum(counts)[:, None, None]
    same = jnp.all((first + row >= ends) == (first + owner >= ends), axis=0)
    inside = (owner >= 2 * HALF) & (owner < 2 * HALF + frames)
    valid = (first + row >= 0) & (first + row < limit)
    return (same & inside & valid).astype(jnp.bfloat16)


def shift_copies(source, copies):
    rows = copies.shape[1]
    for b in range(SUB):
        copies[b] = source[b : b + rows]


def lane_groups():
    tiles = [pl.ds(t * LANES, LANES) for t in range(TILE // LANES)]
    return [tiles[t : t + GROUP] for t in range(0, len(tiles), GROUP)]


def convolve(ids_ref, ids, copies, taps_ref, out_ref, rows, centre, tap_of, id_shift):
    offsets = [o for o in range(KERNEL + 1) if 0 <= tap_of(o) < KERNEL]
    for tiles in lane_groups():
        def step(j, carry, tiles=tiles):
            base = pl.multiple_of(j * SUB * BLOCKS, SUB * BLOCKS)
            own = [ids_ref[pl.ds(base + i * SUB + centre, SUB), :] for i in range(BLOCKS)]
            totals = [[jnp.zeros((SUB, LANES), F32) for _ in tiles] for _ in range(BLOCKS)]
            for low in range(SUB):
                steps = [o // SUB for o in offsets if o % SUB == low]
                reads = range(min(steps), max(steps) + BLOCKS)
                near = {i: ids[low, pl.ds(base + i * SUB + id_shift, SUB), :] for i in reads}
                keep = {(a, i): near[a + i] == own[i] for a in steps for i in range(BLOCKS)}
                for t, lanes in enumerate(tiles):
                    value = {i: copies[low, pl.ds(base + i * SUB, SUB), lanes] for i in reads}
                    for a in steps:
                        tap = taps_ref[pl.ds(tap_of(a * SUB + low), 1), lanes]
                        for i in range(BLOCKS):
                            term = jnp.where(keep[a, i], value[a + i], 0.0)
                            totals[i][t] = totals[i][t] + tap * term
            for i in range(BLOCKS):
                for t, lanes in enumerate(tiles):
                    out_ref[pl.ds(base + i * SUB, SUB), lanes] = totals[i][t]
            return carry

        lax.fori_loop(0, rows // (SUB * BLOCKS), step, 0)


def correlate(grad_ref, ids_ref, ids, copies, rows, first, out_ref):
    steps = range(KERNEL // SUB)
    for tiles in lane_groups():
        for low in range(SUB):
            def step(j, sums, tiles=tiles, low=low):
                base = pl.multiple_of(j * SUB * BLOCKS, SUB * BLOCKS)
                reads = range(len(steps) + BLOCKS - 1)
                own = [ids_ref[pl.ds(base + i * SUB + first + HALF, SUB), :] for i in range(BLOCKS)]
                near = [ids[low, pl.ds(base + i * SUB + first, SUB), :] for i in reads]
                keep = {(a, i): near[a + i] == own[i] for a in steps for i in range(BLOCKS)}
                out = list(sums)
                for t, lanes in enumerate(tiles):
                    value = [copies[low, pl.ds(base + i * SUB + first, SUB), lanes] for i in reads]
                    grads = [grad_ref[pl.ds(base + i * SUB, SUB), lanes] for i in range(BLOCKS)]
                    for a in steps:
                        at = t * len(steps) + a
                        for i in range(BLOCKS):
                            out[at] = out[at] + jnp.where(keep[a, i], value[a + i], 0.0) * grads[i]
                return tuple(out)

            start = tuple(jnp.zeros((SUB, LANES), F32) for _ in range(len(steps) * len(tiles)))
            sums = lax.fori_loop(0, rows // (SUB * BLOCKS), step, start)
            for t, lanes in enumerate(tiles):
                for a in steps:
                    total = jnp.sum(sums[t * len(steps) + a], axis=0, keepdims=True)
                    out_ref[pl.ds(a * SUB + low, 1), lanes] = total


def prepare(low_ref, mid_ref, high_ref, ids_ref, copies, ids):
    @pl.when(pl.program_id(0) == 0)
    def _():
        shift_copies(ids_ref[...], ids)

    parts = [low_ref[...][: 2 * HALF], mid_ref[...], high_ref[...][: 2 * HALF]]
    shift_copies(jnp.concatenate([p.astype(F32) for p in parts]), copies)


def conv_kernel(low_ref, mid_ref, high_ref, ids_ref, taps_ref, conv_ref, stats_ref, sent_ref, copies, ids):
    rows = conv_ref.shape[0]
    prepare(low_ref, mid_ref, high_ref, ids_ref, copies, ids)
    convolve(ids_ref, ids, copies, taps_ref, conv_ref, rows, HALF, lambda o: o, 0)
    inner = conv_ref[HALF : rows - HALF, :]
    mean = jnp.sum(inner, axis=0, keepdims=True) / inner.shape[0]
    stats = jnp.concatenate([mean, jnp.sum(jnp.square(inner - mean), axis=0, keepdims=True)])
    stats_ref[...] = stats
    sent_ref[...] = jnp.broadcast_to(stats[None], sent_ref.shape)


def moments_kernel(
    low_ref, mid_ref, high_ref, ids_ref, conv_ref, stats_ref, out_ref, copies, ids, centred
):
    rows = conv_ref.shape[0] - 2 * HALF
    prepare(low_ref, mid_ref, high_ref, ids_ref, copies, ids)
    centred[...] = conv_ref[HALF : HALF + rows, :] - stats_ref[0:1, :]
    correlate(centred, ids_ref, ids, copies, rows, HALF, out_ref)


def act_kernel(
    count, core_ref, low_ref, mid_ref, high_ref, ids_ref, conv_ref, back_ref, all_ref, own_ref, affine_ref,
    plain_ref, product_ref, swished_ref, grad_ref, kept_ref, given_ref, norm_ref, copies, ids, centred, taps,
):
    rows = conv_ref.shape[0] - 2 * HALF
    prepare(low_ref, mid_ref, high_ref, ids_ref, copies, ids)
    merge = all_ref.shape[0]
    means = [all_ref[i, 0:1, :] for i in range(merge)]
    mean = sum(means) / merge
    spread = sum(jnp.square(m - mean) for m in means)
    var = (sum(all_ref[i, 1:2, :] for i in range(merge)) + count * spread) / (count * merge)
    inverse = lax.rsqrt(var + EPSILON)
    norm_ref[...] = jnp.concatenate([mean, inverse])
    normed = (conv_ref[...] - mean) * inverse
    act = affine_ref[0:1, :] * normed + affine_ref[1:2, :]
    gate = jax.nn.sigmoid(act)
    grad = back_ref[...] * gate * (1.0 + act * (1.0 - gate))
    grad_ref[...] = grad
    swished_ref[...] = (act * gate)[HALF : HALF + rows].astype(jnp.bfloat16)
    inner, inner_normed = grad[HALF : HALF + rows], normed[HALF : HALF + rows]
    sums = [jnp.sum(inner, axis=0, keepdims=True), jnp.sum(inner * inner_normed, axis=0, keepdims=True)]
    centred[...] = inner
    correlate(centred, ids_ref, ids, copies, rows, HALF, taps)
    plain = plain_ref[...]
    product = inverse * (product_ref[...] + (own_ref[0:1, :] - mean) * plain)
    chips = kept_ref.shape[0]
    first = core_ref[0] == 0
    for i in range(chips):
        low, high = (
            jnp.concatenate([v[at : at + 1] for v in (taps, plain, product)] + [sums[at // chips]])
            for at in (i, chips + i)
        )
        kept_ref[i] = jnp.where(first, low, high)
        given_ref[i] = jnp.where(first, high, low)


def weight_kernel(_, own_ref, other_ref, own_grad_ref, other_grad_ref, left_ref, right_ref):
    over = (((0,), (0,)), ((), ()))
    part = lax.dot_general(own_ref[...], own_grad_ref[...], over, preferred_element_type=F32)
    part = part + lax.dot_general(other_ref[...], other_grad_ref[...], over, preferred_element_type=F32)
    part = part.astype(jnp.bfloat16)
    each, left = left_ref.shape[1:]
    for i in range(left_ref.shape[0]):
        left_ref[i] = part[i * each : (i + 1) * each, :left]
        right_ref[i, 0:each, :] = part[i * each : (i + 1) * each, left:]


def tap_kernel(total_rows, parts_ref, sums_ref, norm_ref, affine_ref, _, out_ref):
    scale = affine_ref[0:1, :] * norm_ref[1:2, :]
    shift, slope = sums_ref[0:1, :] / total_rows, sums_ref[1:2, :] / total_rows
    rest = scale * (parts_ref[0:1, :] - shift * parts_ref[1:2, :] - slope * parts_ref[2:3, :])
    height, size = out_ref.shape[1:]
    rows = []
    for _ in range(2):
        term = rest.astype(jnp.bfloat16).astype(F32)
        rows += [term[:, at : at + size] for at in range(0, rest.shape[1], size)]
        rest = rest - term
    rows.append(jnp.zeros((height - len(rows), size), F32))
    rows = jnp.concatenate(rows).astype(jnp.bfloat16)
    for i in range(out_ref.shape[0]):
        out_ref[i] = rows


def collect_kernel(left_ref, right_ref, out_ref, taps_ref):
    each = out_ref.shape[1]
    rows, left = left_ref.shape[1:]
    size = right_ref.shape[2]
    for all_ref, columns in ((left_ref, slice(0, left)), (right_ref, slice(left, left + size))):
        total = sum(all_ref[i, 0:rows, :].astype(F32) for i in range(all_ref.shape[0]))
        for i in range(out_ref.shape[0]):
            out_ref[i, :, columns] = total[i * each : (i + 1) * each].astype(out_ref.dtype)
    pieces = taps_ref.shape[1] // size
    for i in range(right_ref.shape[0]):
        terms = right_ref[i, rows:, :].astype(F32)
        terms = terms[:pieces] + terms[pieces : 2 * pieces]
        for piece in range(pieces):
            taps_ref[i : i + 1, piece * size : (piece + 1) * size] = terms[piece : piece + 1]


def frame_kernel(
    total_rows, ids_ref, conv_ref, grad_ref, norm_ref, sums_ref, affine_ref, taps_ref, out_ref, copies, ids, result
):
    rows = out_ref.shape[0]

    @pl.when(pl.program_id(0) == 0)
    def _():
        shift_copies(ids_ref[...], ids)

    mean, inverse = norm_ref[0:1, :], norm_ref[1:2, :]
    scale = affine_ref[0:1, :] * inverse
    shift, slope = sums_ref[0:1, :] / total_rows, sums_ref[1:2, :] / total_rows
    normed = (conv_ref[...] - mean) * inverse
    grad = scale * (grad_ref[...] - shift - normed * slope)
    for b in range(SUB):
        count = rows + 2 * HALF - (SUB if b else 0)
        copies[b, 0:count, :] = grad[b : b + count]

    convolve(
        ids_ref, ids, copies, taps_ref, result, rows, 2 * HALF, lambda o: KERNEL - o, HALF
    )
    out_ref[...] = result[...].astype(jnp.bfloat16)


PARAMS = pltpu.CompilerParams(vmem_limit_bytes=12 * 1024 * 1024)


def cut(shape, width):
    lead = (0,) * (len(shape) - 1)
    if shape == (1,):
        return pl.BlockSpec(memory_space=pltpu.SMEM)
    if shape[-1] != width:
        return pl.BlockSpec(shape, lambda i: lead + (0,))
    return pl.BlockSpec(shape[:-1] + (TILE,), lambda i: lead + (i,))


def call(kernel, width, ins, outs, scratch, weight=1):
    return pl.pallas_call(
        kernel,
        grid=(width // TILE,),
        in_specs=[cut(a.shape, width) for a in ins],
        out_specs=[cut(shape, width) for shape, _ in outs],
        out_shape=[jax.ShapeDtypeStruct(shape, kind) for shape, kind in outs],
        scratch_shapes=scratch,
        compiler_params=PARAMS,
        cost_estimate=pl.CostEstimate(
            flops=weight * 192 * KERNEL * width * 4, bytes_accessed=4 * 224 * width * 4, transcendentals=0
        ),
    )(*ins)


def local(frame_counts, glu_out, tap_weight, bn_gain, bn_shift, proj_weight, out_grad):
    inputs = glu_out[0]
    grads_in = out_grad[0]
    frames, width = inputs.shape
    half_width = width // 2
    devices = lax.axis_size(SEQ)
    chips, column = lax.axis_size(PLANE), lax.axis_size(COLUMN)
    total_rows = frames * chips * column
    core = lax.axis_index("c")
    rows = frames + 2 * HALF
    reach = frames + 4 * HALF - SUB
    bf16 = jnp.bfloat16

    up = jnp.concatenate([inputs[-2 * HALF :], grads_in[-HALF:]])
    down = jnp.concatenate([inputs[: 2 * HALF], grads_in[:HALF]])
    low, high = shifted(up, SEQ, 1), shifted(down, SEQ, -1)
    grads_wide = jnp.concatenate([low[2 * HALF :], grads_in, high[2 * HALF :]])

    first = lax.axis_index(SEQ) * frames - 2 * HALF
    positions = first + jnp.arange(frames + 4 * HALF, dtype=jnp.int32)
    segments = segment_ids(frame_counts[0], positions, frames * devices)
    segments = jnp.broadcast_to(segments[:, None], (frames + 4 * HALF, LANES))
    value_copies = pltpu.VMEM((SUB, reach, TILE), F32)
    id_copies = pltpu.VMEM((SUB, reach, LANES), jnp.int32)
    column_rows = pltpu.VMEM((frames, TILE), F32)

    conv, own_stats, sent = call(
        conv_kernel, width, [low, inputs, high, segments, tap_weight],
        [((rows, width), F32), ((2, width), F32), ((chips, 2, width), F32)],
        [value_copies, id_copies],
    )
    back = lax.dot_general(
        grads_wide, proj_weight, (((1,), (1,)), ((), ())), preferred_element_type=F32
    )
    own_stats, bn_gain, bn_shift = lax.optimization_barrier((own_stats, bn_gain, bn_shift))
    affine = jnp.stack([bn_gain, bn_shift])
    sent, back, grads_in = lax.optimization_barrier((exchanged(sent, PLANE), back, grads_in))
    stats, conv = lax.optimization_barrier((merged(sent, frames), conv))
    (product,) = call(
        moments_kernel, width, [low, inputs, high, segments, conv, own_stats], [((KERNEL, width), F32)],
        [value_copies, id_copies, column_rows],
    )
    wide = jnp.concatenate([low[: 2 * HALF], inputs, high[: 2 * HALF]])
    plain = jnp.dot(
        window_mask(frame_counts[0], first, frames, frames * devices), wide, preferred_element_type=F32
    )
    stats = gathered(stats, COLUMN)

    swished, act_grad, kept, given, norm = call(
        functools.partial(act_kernel, frames * chips), width,
        [core.reshape(1), low, inputs, high, segments, conv, back, stats, own_stats, affine, plain, product],
        [((frames, width), bf16), ((rows, width), F32), ((chips, 4, width), F32), ((chips, 4, width), F32),
         ((2, width), F32)],
        [value_copies, id_copies, column_rows, pltpu.VMEM((KERNEL, TILE), F32)],
    )
    sent, swished = lax.optimization_barrier((kept + rotated(given, "c", 1), swished))
    sent = exchanged(sent, PLANE)

    share = width // chips
    right_width = half_width // 3
    left_width = half_width - right_width
    height = share + 16
    left, right = pl.pallas_call(
        weight_kernel,
        grid_spec=pltpu.PrefetchScalarGridSpec(
            num_scalar_prefetch=1,
            grid=(4,),
            in_specs=[pl.BlockSpec((frames, width // 4), lambda i, own: (0, i))] * 2
            + [pl.BlockSpec((frames, half_width), lambda i, own: (0, own[0]))] * 2,
            out_specs=[
                pl.BlockSpec((chips // 4, share, left_width), lambda i, own: (i, 0, 0)),
                pl.BlockSpec((chips // 4, height, right_width), lambda i, own: (i, 0, 0)),
            ],
        ),
        out_shape=[
            jax.ShapeDtypeStruct((chips, share, left_width), bf16),
            jax.ShapeDtypeStruct((chips, height, right_width), bf16),
        ],
        compiler_params=PARAMS,
        cost_estimate=pl.CostEstimate(
            flops=4 * frames * width * half_width, bytes_accessed=6 * width * half_width, transcendentals=0
        ),
    )(core.reshape(1), swished, rotated(swished, "c", 1), grads_in, rotated(grads_in, "c", 1))
    block = jnp.dot(swished, proj_weight, preferred_element_type=F32).astype(bf16)
    sent, left, right = lax.optimization_barrier((sent, left, right))
    left = exchanged(left, PLANE)

    sent = jnp.sum(sent, axis=0)
    bit = 1
    while bit < lax.axis_size("z"):
        sent = sent + crossed(sent, "z", bit)
        bit *= 2
    sums = doubled(sent[3:], "c", 1)
    sums, sent, left, right = lax.optimization_barrier((sums, sent, left, right))
    right = pl.pallas_call(
        functools.partial(tap_kernel, total_rows),
        grid=(1,),
        in_specs=[cut(a.shape, 0) for a in (sent, sums, norm, affine)] + [pl.BlockSpec(memory_space=pl.ANY)],
        out_specs=pl.BlockSpec((chips, height - share, right_width), lambda i: (0, share // (height - share), 0)),
        out_shape=jax.ShapeDtypeStruct(right.shape, bf16),
        input_output_aliases={4: 0},
        compiler_params=PARAMS,
    )(sent, sums, norm, affine, right)
    right = exchanged(right, PLANE)

    (frame_grad,) = call(
        functools.partial(frame_kernel, total_rows), width,
        [segments, conv, act_grad, norm, sums, affine, tap_weight], [((frames, width), bf16)],
        [value_copies, id_copies, column_rows],
    )
    right, frame_grad, block = lax.optimization_barrier((right, frame_grad, block))
    part, tap_grad = pl.pallas_call(
        collect_kernel,
        grid=(1,),
        in_specs=[cut(left.shape, 0), cut(right.shape, 0)],
        out_specs=[cut((column, share // column, half_width), 0), cut((chips, width), 0)],
        out_shape=[
            jax.ShapeDtypeStruct((column, share // column, half_width), bf16),
            jax.ShapeDtypeStruct((chips, width), F32),
        ],
        compiler_params=PARAMS,
    )(left, right)
    tap_grad = doubled(tap_grad, "c", 1)
    part = exchanged(part, COLUMN).astype(F32)
    part = jnp.sum(part.reshape((2, column // 2) + part.shape[1:]), axis=1)
    proj_grad = jnp.concatenate([part[0], part[1]], axis=1)
    return (block[None], frame_grad[None], tap_grad, sums[1], sums[0], proj_grad)


def solution(mesh):
    grid = Mesh(mesh.devices.reshape(4, 4, 2, -1), ("x", "y", "c", "z"))
    wide = P("z", SEQ, None)
    return jax.shard_map(
        local,
        mesh=grid,
        in_specs=(P("z", None), wide, P(), P(), P(), P(), wide),
        out_specs=(wide, wide, P(), P(), P(), P(("x", "y", "c", "z"), None)),
        check_vma=False,
    )
```
